512 devices in a mesh: gx: 64 (over z, x, core), gy: 8 (over y).
Axes of the slice: x: 4, y: 8, z: 8, core: 2. Of those that a mesh axis runs over, the one named last changes fastest.
Arguments:
- material_fraction: float32 [256, 128, 256], P('gx', 'gy'), may hold values from 0.02 to 0.98
- primal_warmth: float32 [256, 128, 256], P('gx', 'gy'), may hold values from 0 to 7, as said below
- empty_region_flags: int32 [256, 128, 256], P('gx', 'gy'), may hold values 0 or 1
- dirichlet_flags: int32 [256, 128, 256], P('gx', 'gy'), may hold values 0 or 1
Outputs:
- dual_field_final: float32 [256, 128, 256], P('gx', 'gy')
- sensitivity: float32 [256, 128, 256], P('gx', 'gy')
The draws below stay inside these ranges and needn't reach their ends.
Inputs may be any that keep to these rules, and one draw needn't show every extreme that they name: `primal_warmth`: positive temperatures.
All inputs are finite; a program needn't handle non-finite values. No bound on the sum of `empty_region_flags` or of `dirichlet_flags` on one device may be relied on, other than what follows from the above.
Results may differ from the reference program's by a relative error of at most 0.003.
Values sent between devices are 32-bit elements; how exact they have to be, the bound alone decides.
No kernel may reach another device: no remote copies, remote signals or barrier semaphores. Data moves between devices by JAX's collectives and lax.ppermute only.
A program may use at most 64 MiB of HBM per device.

```python
import math
import jax
import jax.numpy as jnp

ITERS = 3
NX = 256
NY = 128
NZ = 256


def draw_primal_warmth(key, part):
    key = jax.random.fold_in(key, 5)
    ramp = 1.0 + 2.0 * jnp.arange(NX, dtype=jnp.float32) / (NX - 1)
    base = jax.random.uniform(key, (NX, NY, NZ), jnp.float32, 0.5, 1.5)
    return base * ramp[:, None, None]


def with_ends(entries, key, low, largest):
    index_at = [jax.random.randint(jax.random.fold_in(key, axis), (), 0, length) for axis, length in enumerate(entries.shape)]
    longest = entries.shape.index(max(entries.shape))
    beside = index_at[:longest] + [(index_at[longest] + 1) % entries.shape[longest]] + index_at[longest + 1:]
    return entries.at[tuple(index_at)].set(low).at[tuple(beside)].set(largest)


def block_levels(rng, dims, shards, low, largest):
    factor_of = 1.0
    for position, blocks in shards:
        draws = jax.random.uniform(jax.random.fold_in(jax.random.fold_in(rng, 6), position), (blocks,), jnp.float32, low / len(shards), largest / len(shards))
        factor_of = factor_of * jnp.repeat(jnp.exp(draws), dims[position] // blocks).reshape((-1,) + (1,) * (len(dims) - 1 - position))
    return factor_of


def setup_inputs(seed: int = 0) -> dict:
    key_list = jax.random.split(jax.random.key(seed), 5)
    return {
        "material_fraction": jnp.clip(0.02 + 0.96000002 * jax.random.uniform(key_list[0], (NX, NY, NZ), jnp.float32) ** block_levels(key_list[0], (NX, NY, NZ), ((0, 64), (1, 8)), -0.2, 0.2), 0.02, 0.98),
        "primal_warmth": draw_primal_warmth(jax.random.fold_in(key_list[4], 71), 0),
        "empty_region_flags": with_ends((jax.random.randint(key_list[2], (NX, NY, NZ), 0, 2) < 1).astype(jnp.int32), jax.random.fold_in(key_list[2], 1), 0, 1),
        "dirichlet_flags": with_ends((jax.random.randint(key_list[3], (NX, NY, NZ), 0, 8) < 1).astype(jnp.int32), jax.random.fold_in(key_list[3], 1), 0, 1),
    }


KMIN = 0.05
QZERO = 1.0

def filter_taps():
    taps = []
    for dx in (-1, 0, 1):
        for dy in (-1, 0, 1):
            for dz in (-1, 0, 1):
                count = abs(dx) + abs(dy) + abs(dz)
                if count < 3:
                    weight = 1.5 if count == 0 else 0.5 if count == 1 else 1.5 - math.sqrt(2.0)
                    taps.append((dx, dy, dz, weight))
    return taps

def lift(arr):
    return jnp.concatenate([arr[..., 1:], jnp.zeros_like(arr[..., :1])], axis=-1)

def lower_z(arr):
    return jnp.concatenate([jnp.zeros_like(arr[..., :1]), arr[..., :-1]], axis=-1)

def along_z(arr, step):
    if step == 1:
        return lift(arr)
    if step == -1:
        return lower_z(arr)
    return arr

def filter_sum(padded, start, element_columns, element_row_count):
    total = None
    for dx, dy, dz, weight in filter_taps():
        piece = along_z(padded[start + dx:start + dx + element_columns, start + dy:start + dy + element_row_count], dz)
        total = weight * piece if total is None else total + weight * piece
    return total

def vertex_values(padded, start, element_columns, element_row_count):
    corners = {}
    for a in (0, 1):
        for b in (0, 1):
            base = padded[start + a:start + a + element_columns, start + b:start + b + element_row_count]
            corners[a, b, 0] = base
            corners[a, b, 1] = lift(base)
    return corners

def conductance_operator(corners):
    total = sum(corners.values())
    result = {}
    for (a, b, c), value in corners.items():
        near = corners[1 - a, b, c] + corners[a, 1 - b, c] + corners[a, b, 1 - c]
        result[a, b, c] = (5.0 * value + near - total) / 12.0
    return result

def assemble(weight, parts, element_columns, element_row_count):
    total = None
    for (a, b, c), value in parts.items():
        piece = along_z((weight * value)[1 - a:1 - a + element_columns, 1 - b:1 - b + element_row_count], -c)
        total = piece if total is None else total + piece
    return total

def reference(material_fraction, primal_warmth, empty_region_flags, dirichlet_flags):
    element_columns, element_row_count, nz = material_fraction.shape
    movable_points = (1 - dirichlet_flags).astype(jnp.float32)
    fixed = dirichlet_flags.astype(jnp.float32)
    thermal_forcing = empty_region_flags.astype(jnp.float32)
    side = ((1, 1), (1, 1), (0, 0))
    hs = filter_sum(jnp.pad(jnp.ones_like(material_fraction), side), 1, element_columns, element_row_count)
    rho = filter_sum(jnp.pad(material_fraction, side), 1, element_columns, element_row_count) / hs
    solid = 1.0 - rho
    conduct = KMIN + (1.0 - KMIN) * solid ** 3
    slope_k = -3.0 * (1.0 - KMIN) * solid ** 2
    slope_q = -3.0 * QZERO * solid ** 2
    lower = ((1, 0), (1, 0), (0, 0))
    conduct_pad = jnp.pad(conduct, lower)
    ones = {(a, b, c): jnp.ones_like(conduct_pad) for a in (0, 1) for b in (0, 1) for c in (0, 1)}
    diag = movable_points * assemble(conduct_pad / 3.0, ones, element_columns, element_row_count) + fixed

    def operate(field):
        padded = jnp.pad(movable_points * field, side)
        local = conductance_operator(vertex_values(padded, 0, element_columns + 1, element_row_count + 1))
        return movable_points * assemble(conduct_pad, local, element_columns, element_row_count) + fixed * field
    forcing_vector = thermal_forcing * movable_points * primal_warmth
    dual_field_final = jnp.zeros_like(forcing_vector)
    residual = forcing_vector
    precond = residual / diag
    direction = precond
    rz_now = jnp.sum(residual * precond)
    for step in range(ITERS):
        image = operate(direction)
        alpha = rz_now / jnp.sum(direction * image)
        dual_field_final = dual_field_final + alpha * direction
        residual = residual - alpha * image
        if step + 1 < ITERS:
            precond = residual / diag
            rz_next = jnp.sum(residual * precond)
            direction = precond + rz_next / rz_now * direction
            rz_now = rz_next
    ceiling_limit = ((0, 1), (0, 1), (0, 0))
    vertex_warmth = vertex_values(jnp.pad(movable_points * primal_warmth, ceiling_limit), 0, element_columns, element_row_count)
    adj_corners = vertex_values(jnp.pad(dual_field_final, ceiling_limit), 0, element_columns, element_row_count)
    thermal_load = conductance_operator(vertex_warmth)
    energy = sum((adj_corners[key] * thermal_load[key] for key in thermal_load))
    adj_total = sum(adj_corners.values())
    srho = -slope_k * energy + slope_q / 8.0 * adj_total
    sensitivity = filter_sum(jnp.pad(srho / hs, side), 1, element_columns, element_row_count)
    return (dual_field_final, sensitivity)
```

```python
import functools
import math

import jax
import jax.numpy as jnp
from jax import lax
from jax.experimental import pallas as pl
from jax.experimental.pallas import tpu as pltpu
from jax.sharding import PartitionSpec as P

KMIN = 0.05
QZERO = 1.0
EDGE = 0.5
DIAGONAL = 1.5 - math.sqrt(2.0)

WIDE = 8
NEAR = 4
BASIS = 3
MOMENTS = 8


def up(arr, axis):
    return pltpu.roll(arr, arr.shape[axis] - 1, axis)


def down(arr, axis):
    return pltpu.roll(arr, 1, axis)


def z_index(arr):
    return lax.broadcasted_iota(jnp.int32, arr.shape, 1)


def lift(arr):
    return jnp.where(z_index(arr) == arr.shape[1] - 1, 0.0, up(arr, 1))


def lower_z(arr):
    return jnp.where(z_index(arr) == 0, 0.0, down(arr, 1))


def filtered(below, here, above):
    beside = below + above
    rim = up(here, 0) + down(here, 0)
    corner = up(beside, 0) + down(beside, 0)
    flat = 1.5 * here + EDGE * (beside + rim) + DIAGONAL * corner
    slanted = EDGE * here + DIAGONAL * (beside + rim)
    return flat + lift(slanted) + lower_z(slanted)


def grid_flags(layer, layers, first_layer, first_row, rows, shape):
    def inside(at):
        return ((at >= 0) & (at < layers)).astype(jnp.float32)

    at = first_layer + layer
    row = first_row + lax.broadcasted_iota(jnp.int32, shape, 0)

    def row_inside(offset):
        return ((row + offset >= 0) & (row + offset < rows)).astype(jnp.float32)

    return inside(at), inside(at - 1) + inside(at + 1), row_inside(0), row_inside(-1) + row_inside(1)


def filter_weight(layer, layers, first_layer, first_row, rows, shape):
    here, beside, row_here, row_beside = grid_flags(
        layer, layers, first_layer, first_row, rows, shape
    )
    z = lax.broadcasted_iota(jnp.int32, shape, 1)
    z_beside = (z > 0).astype(jnp.float32) + (z < shape[1] - 1).astype(jnp.float32)
    flat = (1.5 + EDGE * beside) * row_here + (EDGE + DIAGONAL * beside) * row_beside
    slanted = (EDGE + DIAGONAL * beside) * row_here + DIAGONAL * row_beside
    valid = here * row_here
    return valid, jnp.where(valid > 0, flat + z_beside * slanted, 1.0)


def yz_modes(node):
    lifted = lift(node)
    plain, slope = node + lifted, lifted - node
    plain_up, slope_up = up(plain, 0), up(slope, 0)
    return plain + plain_up, slope + slope_up, plain_up - plain, slope_up - slope


def element_modes(low, high):
    return {
        "d0": (3.0, high[0] - low[0]),
        "s1": (3.0, high[1] + low[1]),
        "s2": (3.0, high[2] + low[2]),
        "d1": (2.0, high[1] - low[1]),
        "d2": (2.0, high[2] - low[2]),
        "s3": (2.0, high[3] + low[3]),
        "d3": (1.0, high[3] - low[3]),
    }


def apply_layers(node_at, conduct_at, first, count):
    low = yz_modes(node_at(first - 1))
    carried = None
    for element in range(first - 1, first + count):
        high = yz_modes(node_at(element + 1))
        scaled = conduct_at(element) * (1.0 / 48.0)
        flow = {key: (order * value) * scaled for key, (order, value) in element_modes(low, high).items()}
        zero_sum = flow["d0"]
        if carried is not None:
            planes = (
                carried[0] - zero_sum,
                carried[1] + (flow["s1"] - flow["d1"]),
                carried[2] + (flow["s2"] - flow["d2"]),
                carried[3] + (flow["s3"] - flow["d3"]),
            )
            smooth = (planes[0] - planes[2]) + down(planes[0] + planes[2], 0)
            slope = (planes[1] - planes[3]) + down(planes[1] + planes[3], 0)
            yield element, (smooth - slope) + lower_z(smooth + slope)
        carried = (
            zero_sum,
            flow["s1"] + flow["d1"],
            flow["s2"] + flow["d2"],
            flow["s3"] + flow["d3"],
        )
        low = high


def tile_sum(value):
    return functools.reduce(
        jnp.add,
        [
            value[r : r + 8, c : c + 128]
            for r in range(0, value.shape[0], 8)
            for c in range(0, value.shape[1], 128)
        ],
    )


def basis_kernel(
    n, own_rows, layers, rows,
    design_ref, free_ref, rhs_ref, lo_ref, hi_ref, below_ref, above_ref,
    moments_ref, basis_ref, solid_ref,
    conduct_s, diag_s, inv_s, u0_s, u1_s,
):
    first_layer = lax.axis_index("gx") * n
    first_row = lax.axis_index("gy") * own_rows
    wide_rows = own_rows + 2 * WIDE
    near_rows = own_rows + 2 * NEAR
    wide_tiles, near_tiles = wide_rows // 8, near_rows // 8
    z = design_ref.shape[-1]

    def design_at(i):
        if i == -n - 1:
            return below_ref[0]
        if i == 2 * n:
            return above_ref[0]
        if 0 <= i < n:
            return design_ref[i]
        ref, at = (lo_ref, i + n) if i < 0 else (hi_ref, i - n)
        return ref[at * wide_tiles : (at + 1) * wide_tiles].reshape(wide_rows, z)

    def node_at(which, own_ref):
        def at(i):
            if 0 <= i < n:
                return own_ref[i]
            if i < 0:
                start = n * wide_tiles + (which * (n - 1) + i + n - 1) * near_tiles
                return lo_ref[start : start + near_tiles].reshape(near_rows, z)
            start = n * wide_tiles + (which * n + i - n) * near_tiles
            return hi_ref[start : start + near_tiles].reshape(near_rows, z)

        return at

    free_at, rhs_at = node_at(0, free_ref), node_at(1, rhs_ref)

    for i in range(-n, 2 * n):
        valid, weight = filter_weight(i, layers, first_layer, first_row - WIDE, rows, (wide_rows, z))
        solid = 1.0 - filtered(design_at(i - 1), design_at(i), design_at(i + 1)) / weight
        solid = solid[WIDE - NEAR : wide_rows - WIDE + NEAR]
        valid = valid[WIDE - NEAR : wide_rows - WIDE + NEAR]
        conduct_s[i + n] = jnp.where(valid > 0, KMIN + (1.0 - KMIN) * (solid * solid * solid), 0.0)
        if -1 <= i <= n:
            solid_ref[i + 1] = solid

    for i in range(1 - n, 2 * n):
        pair = conduct_s[i + n] + conduct_s[i + n - 1]
        pair = pair + down(pair, 0)
        pair = pair + lower_z(pair)
        free = free_at(i)
        diag = free * (pair * (1.0 / 3.0)) + (1.0 - free)
        inverse = 1.0 / diag
        diag_s[i + n - 1] = diag
        inv_s[i + n - 1] = inverse
        u0_s[i + n - 1] = rhs_at(i) * inverse

    row = lax.broadcasted_iota(jnp.int32, (near_rows, z), 0)
    own = (row >= NEAR) & (row < NEAR + own_rows)
    sums = [jnp.zeros((8, 128), jnp.float32) for _ in range(MOMENTS)]

    def gather(which, product):
        sums[which] = sums[which] + tile_sum(jnp.where(own, product, 0.0))

    def conduct_at(i):
        return conduct_s[i + n]

    for i, image in apply_layers(
        lambda i: free_at(i) * u0_s[i + n - 1], conduct_at, 2 - n, 3 * n - 3
    ):
        free, start = free_at(i), u0_s[i + n - 1]
        image = free * image + (1.0 - free) * start
        later = image * inv_s[i + n - 1] - start
        u1_s[i + n - 2] = later
        if -1 <= i <= n + 1:
            basis_ref[0, i + 1] = start
        if 0 <= i < n:
            gather(0, start * image)
            gather(1, later * image)
            gather(5, rhs_at(i) * start)
            gather(6, rhs_at(i) * later)
    for i, image in apply_layers(
        lambda i: free_at(i) * u1_s[i + n - 2], conduct_at, -1, n + 3
    ):
        free, start = free_at(i), u1_s[i + n - 2]
        image = free * image + (1.0 - free) * start
        later = image * inv_s[i + n - 1] - start
        basis_ref[1, i + 1] = start
        basis_ref[2, i + 1] = later
        if 0 <= i < n:
            gather(2, start * image)
            gather(3, later * image)
            gather(7, rhs_at(i) * later)
    low = yz_modes(free_at(0) * basis_ref[2, 1])
    for i in range(n):
        high = yz_modes(free_at(i + 1) * basis_ref[2, i + 2])
        square = sum(order * value * value for order, value in element_modes(low, high).values())
        last = basis_ref[2, i + 1]
        gather(4, square * (conduct_at(i) * (1.0 / 48.0)) + (1.0 - free_at(i)) * last * last)
        low = high

    lane = lax.broadcasted_iota(jnp.int32, (1, 128), 1)
    total = jnp.zeros((1, 128), jnp.float32)
    for k in range(MOMENTS):
        total = total + jnp.where(lane == k, jnp.sum(sums[k], axis=(0, 1), keepdims=True), 0.0)
    moments_ref[...] = jnp.broadcast_to(total, moments_ref.shape)


def sensitivity_kernel(
    n, own_rows, layers, rows,
    basis_ref, solid_ref, warmth_ref, lo_ref, hi_ref,
    parts_ref,
    scaled_s,
):
    first_layer = lax.axis_index("gx") * n
    first_row = lax.axis_index("gy") * own_rows
    near_rows = own_rows + 2 * NEAR
    near_tiles = near_rows // 8
    z = solid_ref.shape[-1]
    shape = (near_rows, z)

    def warmth_at(i):
        if 0 <= i < n:
            return warmth_ref[i]
        if i < 0:
            return lo_ref[lo_ref.shape[0] - near_tiles :].reshape(shape)
        start = hi_ref.shape[0] - (n + 2 - i) * near_tiles
        return hi_ref[start : start + near_tiles].reshape(shape)

    warm_low = yz_modes(warmth_at(-1))
    lows = [yz_modes(basis_ref[k, 0]) for k in range(BASIS)]
    for i in range(-1, n + 1):
        warm_high = yz_modes(warmth_at(i + 1))
        valid, weight = filter_weight(i, layers, first_layer, first_row - NEAR, rows, shape)
        solid = solid_ref[i + 1]
        share = jnp.where(valid > 0, 3.0 * solid * solid / weight, 0.0)
        load = {
            key: (order / 48.0) * value for key, (order, value) in element_modes(warm_low, warm_high).items()
        }
        for k in range(BASIS):
            high = yz_modes(basis_ref[k, i + 2])
            modes = element_modes(lows[k], high)
            energy = sum(load[key] * value for key, (_, value) in modes.items())
            total = lows[k][0] + high[0]
            scaled_s[k, i + 1] = share * ((1.0 - KMIN) * energy - (QZERO / 8.0) * total)
            lows[k] = high
        warm_low = warm_high
    for k in range(BASIS):
        for i in range(n):
            result = filtered(scaled_s[k, i], scaled_s[k, i + 1], scaled_s[k, i + 2])
            parts_ref[k, i] = result[NEAR : NEAR + own_rows]


def final_kernel(n, own_rows, moments_ref, basis_ref, parts_ref, dual_ref, sens_ref):
    total = jnp.sum(moments_ref[...], axis=0, keepdims=True)
    a0, a1, a2, a3, a4, b0, b1, b2 = (
        jnp.broadcast_to(total[:, k : k + 1], (1, 128)) for k in range(MOMENTS)
    )
    l10 = a1 / a0
    l20 = a2 / a0
    d1 = a2 - l10 * a1
    t21 = a3 - l20 * a1
    l21 = t21 / d1
    d2 = a4 - l20 * a2 - l21 * t21
    z1 = b1 - l10 * b0
    z2 = b2 - l20 * b0 - l21 * z1
    y2 = z2 / d2
    y1 = z1 / d1 - l21 * y2
    y0 = b0 / a0 - l10 * y1 - l20 * y2
    z = dual_ref.shape[-1]
    coefs = [jnp.concatenate([y] * (z // 128), axis=1) for y in (y0, y1, y2)]
    for i in range(n):
        dual = sum(coefs[k] * basis_ref[k, i + 1] for k in range(BASIS))
        dual_ref[i] = dual[NEAR : NEAR + own_rows]
        sens_ref[i] = sum(coefs[k] * parts_ref[k, i] for k in range(BASIS))


def shifted(arr, axis, step):
    count = lax.axis_size(axis)
    return lax.ppermute(arr, axis, [(i, i + step) for i in range(count) if 0 <= i + step < count])


def body(gx, gy, material_fraction, primal_warmth, empty_region_flags, dirichlet_flags):
    n, own_rows, z = material_fraction.shape
    layers, rows = gx * n, gy * own_rows
    free = (1 - dirichlet_flags).astype(jnp.float32)
    warmth = free * primal_warmth
    rhs = empty_region_flags.astype(jnp.float32) * warmth
    design = material_fraction

    from_low = shifted(
        jnp.concatenate(
            [design[:, -5:], free[:, -3:], rhs[:, -3:], warmth[:, -1:]], axis=1
        ),
        "gy", 1,
    )
    from_high = shifted(
        jnp.concatenate([design[:, :5], free[:, :4], rhs[:, :4], warmth[:, :2]], axis=1),
        "gy", -1,
    )

    def blank(count):
        return jnp.zeros((n, count, z), jnp.float32)

    design = jnp.concatenate([blank(3), from_low[:, :5], design, from_high[:, :5], blank(3)], axis=1)
    free = jnp.concatenate([blank(1), from_low[:, 5:8], free, from_high[:, 5:9]], axis=1)
    rhs = jnp.concatenate([blank(1), from_low[:, 8:11], rhs, from_high[:, 9:13]], axis=1)
    warmth = jnp.concatenate([blank(3), from_low[:, 11:12], warmth, from_high[:, 13:15], blank(2)], axis=1)

    def tiles(*pieces):
        return jnp.concatenate([p.reshape(-1, 8, z) for p in pieces], axis=0)

    lo = shifted(tiles(design, free[1:], rhs[1:], warmth[n - 1 :]), "gx", 1)
    hi = shifted(tiles(design, free, rhs, warmth[:2]), "gx", -1)
    below = shifted(design[n - 1 :], "gx", 2)
    above = shifted(design[:1], "gx", -2)

    near = own_rows + 2 * NEAR
    f32 = jnp.float32
    inner = min(16, gx)
    outer = gx * gy // inner
    sizes = (n, own_rows, layers, rows)
    moments, basis, solid = pl.pallas_call(
        functools.partial(basis_kernel, *sizes),
        out_shape=(
            jax.ShapeDtypeStruct((inner, 128), f32),
            jax.ShapeDtypeStruct((BASIS, n + 3, near, z), f32),
            jax.ShapeDtypeStruct((n + 2, near, z), f32),
        ),
        scratch_shapes=[
            pltpu.VMEM((3 * n, near, z), f32),
            pltpu.VMEM((3 * n - 1, near, z), f32),
            pltpu.VMEM((3 * n - 1, near, z), f32),
            pltpu.VMEM((3 * n - 1, near, z), f32),
            pltpu.VMEM((3 * n - 3, near, z), f32),
        ],
        name="basis",
    )(design, free, rhs, lo, hi, below, above)

    parts = pl.pallas_call(
        functools.partial(sensitivity_kernel, *sizes),
        out_shape=jax.ShapeDtypeStruct((BASIS, n, own_rows, z), f32),
        scratch_shapes=[pltpu.VMEM((BASIS, n + 2, near, z), f32)],
        name="sensitivity_parts",
        cost_estimate=pl.CostEstimate(flops=40000000, bytes_accessed=2000000, transcendentals=0),
    )(basis, solid, warmth, lo, hi)

    first = [[g * inner + j for j in range(inner)] for g in range(gx // inner)]
    first = [[d * gy + y for d in group] for group in first for y in range(gy)]
    second = [
        [(g * inner + j) * gy + y for g in range(gx // inner) for y in range(gy)]
        for j in range(inner)
    ]
    moments = lax.all_to_all(moments, ("gx", "gy"), 0, 0, axis_index_groups=first, tiled=True)
    moments = jnp.broadcast_to(jnp.sum(moments, axis=0, keepdims=True), (outer, 128))
    moments = lax.all_to_all(moments, ("gx", "gy"), 0, 0, axis_index_groups=second, tiled=True)

    return pl.pallas_call(
        functools.partial(final_kernel, n, own_rows),
        out_shape=(
            jax.ShapeDtypeStruct((n, own_rows, z), f32),
            jax.ShapeDtypeStruct((n, own_rows, z), f32),
        ),
        name="combine",
    )(moments, basis, parts)


def solution(mesh):
    placed = P("gx", "gy", None)
    return jax.shard_map(
        functools.partial(body, mesh.shape["gx"], mesh.shape["gy"]),
        mesh=mesh,
        in_specs=(placed,) * 4,
        out_specs=(placed, placed),
        check_vma=False,
    )
```

```python
import functools
import math

import jax
import jax.numpy as jnp
from jax import lax
from jax.experimental import pallas as pl
from jax.experimental.pallas import tpu as pltpu
from jax.sharding import PartitionSpec as P

KMIN = 0.05
QZERO = 1.0
EDGE = 0.5
DIAGONAL = 1.5 - math.sqrt(2.0)

WIDE = 8
NEAR = 4
BASIS = 3
MOMENTS = 8


def up(arr, axis):
    return pltpu.roll(arr, arr.shape[axis] - 1, axis)


def down(arr, axis):
    return pltpu.roll(arr, 1, axis)


def z_index(arr):
    return lax.broadcasted_iota(jnp.int32, arr.shape, 1)


def lift(arr):
    return jnp.where(z_index(arr) == arr.shape[1] - 1, 0.0, up(arr, 1))


def lower_z(arr):
    return jnp.where(z_index(arr) == 0, 0.0, down(arr, 1))


def filtered(below, here, above):
    beside = below + above
    rim = up(here, 0) + down(here, 0)
    corner = up(beside, 0) + down(beside, 0)
    flat = 1.5 * here + EDGE * (beside + rim) + DIAGONAL * corner
    slanted = EDGE * here + DIAGONAL * (beside + rim)
    return flat + lift(slanted) + lower_z(slanted)


def grid_flags(layer, layers, first_layer, first_row, rows, shape):
    def inside(at):
        return ((at >= 0) & (at < layers)).astype(jnp.float32)

    at = first_layer + layer
    row = first_row + lax.broadcasted_iota(jnp.int32, shape, 0)

    def row_inside(offset):
        return ((row + offset >= 0) & (row + offset < rows)).astype(jnp.float32)

    return inside(at), inside(at - 1) + inside(at + 1), row_inside(0), row_inside(-1) + row_inside(1)


def filter_weight(layer, layers, first_layer, first_row, rows, shape):
    here, beside, row_here, row_beside = grid_flags(
        layer, layers, first_layer, first_row, rows, shape
    )
    z = lax.broadcasted_iota(jnp.int32, shape, 1)
    z_beside = (z > 0).astype(jnp.float32) + (z < shape[1] - 1).astype(jnp.float32)
    flat = (1.5 + EDGE * beside) * row_here + (EDGE + DIAGONAL * beside) * row_beside
    slanted = (EDGE + DIAGONAL * beside) * row_here + DIAGONAL * row_beside
    valid = here * row_here
    return valid, jnp.where(valid > 0, flat + z_beside * slanted, 1.0)


def yz_modes(node):
    lifted = lift(node)
    plain, slope = node + lifted, lifted - node
    plain_up, slope_up = up(plain, 0), up(slope, 0)
    return plain + plain_up, slope + slope_up, plain_up - plain, slope_up - slope


def element_modes(low, high):
    return {
        "d0": (3.0, high[0] - low[0]),
        "s1": (3.0, high[1] + low[1]),
        "s2": (3.0, high[2] + low[2]),
        "d1": (2.0, high[1] - low[1]),
        "d2": (2.0, high[2] - low[2]),
        "s3": (2.0, high[3] + low[3]),
        "d3": (1.0, high[3] - low[3]),
    }


def apply_layers(node_at, conduct_at, first, count):
    low = yz_modes(node_at(first - 1))
    carried = None
    for element in range(first - 1, first + count):
        high = yz_modes(node_at(element + 1))
        scaled = conduct_at(element) * (1.0 / 48.0)
        flow = {key: (order * value) * scaled for key, (order, value) in element_modes(low, high).items()}
        zero_sum = flow["d0"]
        if carried is not None:
            planes = (
                carried[0] - zero_sum,
                carried[1] + (flow["s1"] - flow["d1"]),
                carried[2] + (flow["s2"] - flow["d2"]),
                carried[3] + (flow["s3"] - flow["d3"]),
            )
            smooth = (planes[0] - planes[2]) + down(planes[0] + planes[2], 0)
            slope = (planes[1] - planes[3]) + down(planes[1] + planes[3], 0)
            yield element, (smooth - slope) + lower_z(smooth + slope)
        carried = (
            zero_sum,
            flow["s1"] + flow["d1"],
            flow["s2"] + flow["d2"],
            flow["s3"] + flow["d3"],
        )
        low = high


def tile_sum(value):
    return functools.reduce(
        jnp.add,
        [
            value[r : r + 8, c : c + 128]
            for r in range(0, value.shape[0], 8)
            for c in range(0, value.shape[1], 128)
        ],
    )


def roll_rows(tile, step):
    return pltpu.roll(tile, step % tile.shape[0], 0)


def tiles_of(ref, layer):
    return [ref[layer, r : r + 8] for r in range(0, ref.shape[1], 8)]


def pack_kernel(
    n, material_ref, primal_ref, source_ref, fixed_ref,
    free_ref, rhs_ref, warmth_ref, y_up_ref, y_down_ref, x_up_ref, x_down_ref,
):
    row = lax.broadcasted_iota(jnp.int32, (8, material_ref.shape[-1]), 0)
    for i in range(n):
        free = (1 - fixed_ref[i]).astype(jnp.float32)
        warmth = free * primal_ref[i]
        free_ref[i] = free
        warmth_ref[i] = warmth
        rhs_ref[i] = source_ref[i].astype(jnp.float32) * warmth
        design, free, rhs, warmth = (
            tiles_of(ref, i) for ref in (material_ref, free_ref, rhs_ref, warmth_ref)
        )
        y_up_ref[i] = jnp.where(row >= 3, design[-1], roll_rows(free[-1], 3))
        y_up_ref[n + i] = jnp.where(row >= 5, rhs[-1], roll_rows(warmth[-1], 1))
        y_down_ref[i] = jnp.where(row < 5, design[0], roll_rows(warmth[0], 5))
        y_down_ref[n + i] = jnp.where(row < 4, rhs[0], roll_rows(free[0], 4))
        for ref in (x_up_ref, x_down_ref):
            for t, tile in enumerate(design):
                ref[len(design) * i + t] = tile
    per = material_ref.shape[1] // 8
    spot = per * n
    for ref in (free_ref, rhs_ref):
        for i in range(2, n):
            for tile in tiles_of(ref, i):
                x_up_ref[spot] = tile
                spot += 1
    spot = per * n
    for ref, count in ((free_ref, n - 1), (rhs_ref, n - 1), (warmth_ref, 1)):
        for i in range(count):
            for tile in tiles_of(ref, i):
                x_down_ref[spot] = tile
                spot += 1


def corner_kernel(n, low_ref, high_ref, up_ref, down_ref):
    half = up_ref.shape[0] // 2
    up_ref[:n] = low_ref[:n]
    up_ref[n:half] = low_ref[n + 2 :]
    up_ref[half : half + n] = high_ref[:n]
    up_ref[half + n :] = high_ref[n + 2 :]
    half = down_ref.shape[0] // 2
    down_ref[:n] = low_ref[:n]
    down_ref[n:half] = low_ref[n : 2 * n - 1]
    down_ref[half : half + n] = high_ref[:n]
    down_ref[half + n :] = high_ref[n : 2 * n - 1]


def brick(n, own_rows, own, y_low, y_high, x_low, x_high, corner_low, corner_high):
    design_ref, free_ref, rhs_ref, warmth_ref = own
    per = own_rows // 8

    def rows_of(ref, start):
        return ref[start : start + per].reshape(own_rows, ref.shape[-1])

    def own_part(which, i):
        if 0 <= i < n:
            return own[which][i]
        if i < 0:
            return rows_of(x_low, per * ((i + n) if which == 0 else n + (which - 1) * (n - 2) + i + n - 2))
        return rows_of(x_high, per * ((i - n) if which == 0 else n + (which - 1) * (n - 1) + i - n))

    def y_tile(first, high, i):
        if 0 <= i < n:
            return (y_high if high else y_low)[i if first else n + i]
        ref, at, count = (corner_low, i + n, n - 2) if i < 0 else (corner_high, i - n, n - 1)
        start = (n + count) if high else 0
        if first:
            return ref[start + at]
        return ref[start + n + (i + n - 2 if i < 0 else at)]

    def joined(low, middle, high):
        return jnp.concatenate([low, middle, high], axis=0)

    def near(value):
        return value[WIDE - NEAR : own_rows + WIDE + NEAR]

    def design_at(i):
        return joined(y_tile(True, False, i), own_part(0, i), y_tile(True, True, i))

    def free_at(i):
        return near(
            joined(roll_rows(y_tile(True, False, i), -3), own_part(1, i), roll_rows(y_tile(False, True, i), -4))
        )

    def rhs_at(i):
        return near(joined(y_tile(False, False, i), own_part(2, i), y_tile(False, True, i)))

    def warmth_at(i):
        return near(
            joined(roll_rows(y_tile(False, False, i), -1), own_part(3, i), roll_rows(y_tile(True, True, i), -5))
        )

    return design_at, free_at, rhs_at, warmth_at


def basis_kernel(
    n, own_rows, layers, rows,
    design_ref, free_ref, rhs_ref, y_low, y_high, x_low, x_high, corner_low, corner_high,
    moments_ref, basis_ref, solid_ref,
    conduct_s, free_s, diag_inverse_s, u0_s, u1_s,
):
    first_layer = lax.axis_index("gx") * n
    first_row = lax.axis_index("gy") * own_rows
    wide_rows = own_rows + 2 * WIDE
    near_rows = own_rows + 2 * NEAR
    z = design_ref.shape[-1]
    design_at, free_from, rhs_at, _ = brick(
        n, own_rows, (design_ref, free_ref, rhs_ref, None),
        y_low, y_high, x_low, x_high, corner_low, corner_high,
    )

    for i in range(1 - n, 2 * n - 1):
        valid, weight = filter_weight(i, layers, first_layer, first_row - WIDE, rows, (wide_rows, z))
        solid = 1.0 - filtered(design_at(i - 1), design_at(i), design_at(i + 1)) / weight
        solid = solid[WIDE - NEAR : wide_rows - WIDE + NEAR]
        valid = valid[WIDE - NEAR : wide_rows - WIDE + NEAR]
        conduct_s[i + n - 1] = jnp.where(valid > 0, KMIN + (1.0 - KMIN) * (solid * solid * solid), 0.0)
        if 0 <= i < n:
            solid_ref[i] = solid

    def conduct_at(i):
        return conduct_s[i + n - 1]

    def free_at(i):
        return free_s[i + n - 2]

    for i in range(2 - n, 2 * n - 1):
        pair = conduct_at(i) + conduct_at(i - 1)
        pair = pair + down(pair, 0)
        pair = pair + lower_z(pair)
        free = free_from(i)
        inverse = 1.0 / (free * (pair * (1.0 / 3.0)) + (1.0 - free))
        free_s[i + n - 2] = free
        diag_inverse_s[i + n - 2] = inverse
        u0_s[i + n - 2] = rhs_at(i) * inverse

    row = lax.broadcasted_iota(jnp.int32, (near_rows, z), 0)
    own = (row >= NEAR) & (row < NEAR + own_rows)
    sums = [jnp.zeros((8, 128), jnp.float32) for _ in range(MOMENTS)]

    def gather(which, product):
        sums[which] = sums[which] + tile_sum(jnp.where(own, product, 0.0))

    def step(previous, first, count):
        for i, image in apply_layers(lambda i: free_at(i) * previous(i), conduct_at, first, count):
            free, start = free_at(i), previous(i)
            image = free * image + (1.0 - free) * start
            yield i, start, image, image * diag_inverse_s[i + n - 2] - start

    for i, start, image, later in step(lambda i: u0_s[i + n - 2], 3 - n, 3 * n - 5):
        u1_s[i + n - 3] = later
        if 0 <= i <= n:
            basis_ref[0, i] = start
        if 0 <= i < n:
            rhs = rhs_at(i)
            gather(0, start * image)
            gather(1, later * image)
            gather(5, rhs * start)
            gather(6, rhs * later)
    for i, start, image, later in step(lambda i: u1_s[i + n - 3], 0, n + 1):
        basis_ref[1, i] = start
        basis_ref[2, i] = later
        if i < n:
            gather(2, start * image)
            gather(3, later * image)
            gather(7, rhs_at(i) * later)
    low = yz_modes(free_at(0) * basis_ref[2, 0])
    for i in range(n):
        high = yz_modes(free_at(i + 1) * basis_ref[2, i + 1])
        square = sum(order * value * value for order, value in element_modes(low, high).values())
        last = basis_ref[2, i]
        gather(4, square * (conduct_at(i) * (1.0 / 48.0)) + (1.0 - free_at(i)) * last * last)
        low = high

    lane = lax.broadcasted_iota(jnp.int32, (1, 128), 1)
    total = jnp.zeros((1, 128), jnp.float32)
    for k in range(MOMENTS):
        total = total + jnp.where(lane == k, jnp.sum(sums[k], axis=(0, 1), keepdims=True), 0.0)
    moments_ref[...] = jnp.broadcast_to(total, moments_ref.shape)


def integrand_kernel(
    n, own_rows, layers, rows,
    basis_ref, solid_ref, warmth_ref, y_low, y_high, x_low, x_high, corner_low, corner_high,
    scaled_ref, first_ref, last_ref,
):
    first_layer = lax.axis_index("gx") * n
    first_row = lax.axis_index("gy") * own_rows
    shape = solid_ref.shape[1:]
    *_, warmth_at = brick(
        n, own_rows, (None, None, None, warmth_ref),
        y_low, y_high, x_low, x_high, corner_low, corner_high,
    )
    warm_low = yz_modes(warmth_at(0))
    lows = [yz_modes(basis_ref[k, 0]) for k in range(BASIS)]
    for i in range(n):
        warm_high = yz_modes(warmth_at(i + 1))
        valid, weight = filter_weight(i, layers, first_layer, first_row - NEAR, rows, shape)
        solid = solid_ref[i]
        share = jnp.where(valid > 0, 3.0 * solid * solid / weight, 0.0)
        load = {
            key: (order / 48.0) * value for key, (order, value) in element_modes(warm_low, warm_high).items()
        }
        for k in range(BASIS):
            high = yz_modes(basis_ref[k, i + 1])
            modes = element_modes(lows[k], high)
            energy = sum(load[key] * value for key, (_, value) in modes.items())
            total = lows[k][0] + high[0]
            result = share * ((1.0 - KMIN) * energy - (QZERO / 8.0) * total)
            scaled_ref[k, i] = result
            if i == 0:
                first_ref[k] = result
            if i == n - 1:
                last_ref[k] = result
            lows[k] = high
        warm_low = warm_high


def filter_kernel(n, own_rows, scaled_ref, below_ref, above_ref, parts_ref):
    for k in range(BASIS):
        for i in range(n):
            below = scaled_ref[k, i - 1] if i > 0 else below_ref[k]
            above = scaled_ref[k, i + 1] if i < n - 1 else above_ref[k]
            parts_ref[k, i] = filtered(below, scaled_ref[k, i], above)[NEAR : NEAR + own_rows]


def final_kernel(n, own_rows, moments_ref, basis_ref, parts_ref, dual_ref, sens_ref):
    total = jnp.sum(moments_ref[...], axis=0, keepdims=True)
    a0, a1, a2, a3, a4, b0, b1, b2 = (
        jnp.broadcast_to(total[:, k : k + 1], (1, 128)) for k in range(MOMENTS)
    )
    l10 = a1 / a0
    l20 = a2 / a0
    d1 = a2 - l10 * a1
    t21 = a3 - l20 * a1
    l21 = t21 / d1
    d2 = a4 - l20 * a2 - l21 * t21
    z1 = b1 - l10 * b0
    z2 = b2 - l20 * b0 - l21 * z1
    y2 = z2 / d2
    y1 = z1 / d1 - l21 * y2
    y0 = b0 / a0 - l10 * y1 - l20 * y2
    z = dual_ref.shape[-1]
    coefs = [jnp.concatenate([y] * (z // 128), axis=1) for y in (y0, y1, y2)]
    for i in range(n):
        dual = sum(coefs[k] * basis_ref[k, i] for k in range(BASIS))
        dual_ref[i] = dual[NEAR : NEAR + own_rows]
        sens_ref[i] = sum(coefs[k] * parts_ref[k, i] for k in range(BASIS))


def shifted(arr, axis, step):
    count = lax.axis_size(axis)
    return lax.ppermute(arr, axis, [(i, i + step) for i in range(count) if 0 <= i + step < count])


def in_vmem(count):
    return [pl.BlockSpec(memory_space=pltpu.VMEM)] * count


def body(gx, gy, material_fraction, primal_warmth, empty_region_flags, dirichlet_flags):
    n, own_rows, z = material_fraction.shape
    sizes = (n, own_rows, gx * n, gy * own_rows)
    near = own_rows + 2 * NEAR
    per = own_rows // 8

    def arrays(*shapes):
        return [jax.ShapeDtypeStruct(shape, jnp.float32) for shape in shapes]

    def call(name, kernel, outs, *operands, scratch=(), resident=True, flops=0):
        return pl.pallas_call(
            kernel,
            out_shape=arrays(*outs),
            in_specs=in_vmem(len(operands)) if resident else None,
            out_specs=in_vmem(len(outs)) if resident else None,
            scratch_shapes=[pltpu.VMEM(shape, jnp.float32) for shape in scratch],
            cost_estimate=pl.CostEstimate(flops=flops, bytes_accessed=1 << 20, transcendentals=0),
            name=name,
        )(*operands)

    brick_shape = (n, own_rows, z)
    free, rhs, warmth, y_up, y_down, x_up, x_down = call(
        "pack",
        functools.partial(pack_kernel, n),
        [brick_shape] * 3
        + [(2 * n, 8, z)] * 2
        + [(per * (n + 2 * (n - 2)), 8, z), (per * (n + 2 * (n - 1) + 1), 8, z)],
        material_fraction, primal_warmth, empty_region_flags, dirichlet_flags,
    )
    y_low = shifted(y_up, "gy", 1)
    y_high = shifted(y_down, "gy", -1)
    x_low = shifted(x_up, "gx", 1)
    x_high = shifted(x_down, "gx", -1)
    corner_up, corner_down = call(
        "corners",
        functools.partial(corner_kernel, n),
        [(2 * (2 * n - 2), 8, z), (2 * (2 * n - 1), 8, z)],
        y_low, y_high,
    )
    corner_low = shifted(corner_up, "gx", 1)
    corner_high = shifted(corner_down, "gx", -1)
    halo = (y_low, y_high, x_low, x_high, corner_low, corner_high)

    pairs = 2 if gx % 2 == 0 else 1
    inner, outer = pairs * gy, gx // pairs
    moments, basis, solid = call(
        "basis",
        functools.partial(basis_kernel, *sizes),
        [(inner, 128), (BASIS, n + 1, near, z), (n, near, z)],
        material_fraction, free, rhs, *halo,
        scratch=[
            (3 * n - 2, near, z),
            (3 * n - 3, near, z),
            (3 * n - 3, near, z),
            (3 * n - 3, near, z),
            (3 * n - 5, near, z),
        ],
    )
    scaled, first, last = call(
        "integrand",
        functools.partial(integrand_kernel, *sizes),
        [(BASIS, n, near, z), (BASIS, near, z), (BASIS, near, z)],
        basis, solid, warmth, *halo,
        flops=40000000,
    )
    below = shifted(last, "gx", 1)
    above = shifted(first, "gx", -1)
    (parts,) = call(
        "filter",
        functools.partial(filter_kernel, n, own_rows),
        [(BASIS,) + brick_shape],
        scaled, below, above,
        flops=40000000,
    )

    near_groups = [
        [(g * pairs + c) * gy + y for c in range(pairs) for y in range(gy)] for g in range(outer)
    ]
    far_groups = [
        [(g * pairs + c) * gy + y for g in range(outer)] for c in range(pairs) for y in range(gy)
    ]
    moments = lax.all_to_all(moments, ("gx", "gy"), 0, 0, axis_index_groups=near_groups, tiled=True)
    moments = jnp.broadcast_to(jnp.sum(moments, axis=0, keepdims=True), (outer, 128))
    moments = lax.all_to_all(moments, ("gx", "gy"), 0, 0, axis_index_groups=far_groups, tiled=True)
    return tuple(
        call(
            "combine",
            functools.partial(final_kernel, n, own_rows),
            [brick_shape, brick_shape],
            moments, basis, parts,
        )
    )


def solution(mesh):
    placed = P("gx", "gy", None)
    return jax.shard_map(
        functools.partial(body, mesh.shape["gx"], mesh.shape["gy"]),
        mesh=mesh,
        in_specs=(placed,) * 4,
        out_specs=(placed, placed),
        check_vma=False,
    )
```

```python
import functools
import math

import jax
import jax.numpy as jnp
from jax import lax
from jax.experimental import pallas as pl
from jax.experimental.pallas import tpu as pltpu
from jax.sharding import PartitionSpec as P

KMIN = 0.05
QZERO = 1.0
EDGE = 0.5
DIAGONAL = 1.5 - math.sqrt(2.0)

WIDE = 8
NEAR = 4
BASIS = 3
MOMENTS = 8
VMEM_LIMIT = 12 << 20


def up(arr, axis):
    return pltpu.roll(arr, arr.shape[axis] - 1, axis)


def down(arr, axis):
    return pltpu.roll(arr, 1, axis)


def z_index(arr):
    return lax.broadcasted_iota(jnp.int32, arr.shape, 1)


def lift(arr):
    return jnp.where(z_index(arr) == arr.shape[1] - 1, 0.0, up(arr, 1))


def lower_z(arr):
    return jnp.where(z_index(arr) == 0, 0.0, down(arr, 1))


def filtered(below, here, above):
    beside = below + above
    rim = up(here, 0) + down(here, 0)
    corner = up(beside, 0) + down(beside, 0)
    flat = 1.5 * here + EDGE * (beside + rim) + DIAGONAL * corner
    slanted = EDGE * here + DIAGONAL * (beside + rim)
    return flat + lift(slanted) + lower_z(slanted)


def grid_flags(layer, layers, first_layer, first_row, rows, shape):
    def inside(at):
        return ((at >= 0) & (at < layers)).astype(jnp.float32)

    at = first_layer + layer
    row = first_row + lax.broadcasted_iota(jnp.int32, shape, 0)

    def row_inside(offset):
        return ((row + offset >= 0) & (row + offset < rows)).astype(jnp.float32)

    return inside(at), inside(at - 1) + inside(at + 1), row_inside(0), row_inside(-1) + row_inside(1)


def filter_weight(layer, layers, first_layer, first_row, rows, shape):
    here, beside, row_here, row_beside = grid_flags(
        layer, layers, first_layer, first_row, rows, shape
    )
    z = lax.broadcasted_iota(jnp.int32, shape, 1)
    z_beside = (z > 0).astype(jnp.float32) + (z < shape[1] - 1).astype(jnp.float32)
    flat = (1.5 + EDGE * beside) * row_here + (EDGE + DIAGONAL * beside) * row_beside
    slanted = (EDGE + DIAGONAL * beside) * row_here + DIAGONAL * row_beside
    valid = here * row_here
    return valid, jnp.where(valid > 0, flat + z_beside * slanted, 1.0)


def yz_modes(node):
    lifted = lift(node)
    plain, slope = node + lifted, lifted - node
    plain_up, slope_up = up(plain, 0), up(slope, 0)
    return plain + plain_up, slope + slope_up, plain_up - plain, slope_up - slope


def element_modes(low, high):
    return {
        "d0": (3.0, high[0] - low[0]),
        "s1": (3.0, high[1] + low[1]),
        "s2": (3.0, high[2] + low[2]),
        "d1": (2.0, high[1] - low[1]),
        "d2": (2.0, high[2] - low[2]),
        "s3": (2.0, high[3] + low[3]),
        "d3": (1.0, high[3] - low[3]),
    }


def apply_layers(node_at, conduct_at, first, count):
    low = yz_modes(node_at(first - 1))
    carried = None
    for element in range(first - 1, first + count):
        high = yz_modes(node_at(element + 1))
        scaled = conduct_at(element) * (1.0 / 48.0)
        flow = {key: (order * value) * scaled for key, (order, value) in element_modes(low, high).items()}
        zero_sum = flow["d0"]
        if carried is not None:
            planes = (
                carried[0] - zero_sum,
                carried[1] + (flow["s1"] - flow["d1"]),
                carried[2] + (flow["s2"] - flow["d2"]),
                carried[3] + (flow["s3"] - flow["d3"]),
            )
            smooth = (planes[0] - planes[2]) + down(planes[0] + planes[2], 0)
            slope = (planes[1] - planes[3]) + down(planes[1] + planes[3], 0)
            yield element, (smooth - slope) + lower_z(smooth + slope)
        carried = (
            zero_sum,
            flow["s1"] + flow["d1"],
            flow["s2"] + flow["d2"],
            flow["s3"] + flow["d3"],
        )
        low = high


def tile_sum(value):
    return functools.reduce(
        jnp.add,
        [
            value[r : r + 8, c : c + 128]
            for r in range(0, value.shape[0], 8)
            for c in range(0, value.shape[1], 128)
        ],
    )


def roll_rows(tile, step):
    return pltpu.roll(tile, step % tile.shape[0], 0)


def tiles_of(ref, layer):
    return [ref[layer, r : r + 8] for r in range(0, ref.shape[1], 8)]


def pack_kernel(
    n, material_ref, primal_ref, source_ref, fixed_ref,
    free_ref, rhs_ref, warmth_ref, y_up_ref, y_down_ref, x_up_ref, x_down_ref,
):
    row = lax.broadcasted_iota(jnp.int32, (8, material_ref.shape[-1]), 0)
    for i in range(n):
        free = (1 - fixed_ref[i]).astype(jnp.float32)
        warmth = free * primal_ref[i]
        free_ref[i] = free
        warmth_ref[i] = warmth
        rhs_ref[i] = source_ref[i].astype(jnp.float32) * warmth
        design, free, rhs, warmth = (
            tiles_of(ref, i) for ref in (material_ref, free_ref, rhs_ref, warmth_ref)
        )
        y_up_ref[i] = jnp.where(row >= 3, design[-1], roll_rows(free[-1], 3))
        y_up_ref[n + i] = jnp.where(row >= 5, rhs[-1], roll_rows(warmth[-1], 1))
        y_down_ref[i] = jnp.where(row < 5, design[0], roll_rows(warmth[0], 5))
        y_down_ref[n + i] = jnp.where(row < 4, rhs[0], roll_rows(free[0], 4))
        for ref in (x_up_ref, x_down_ref):
            for t, tile in enumerate(design):
                ref[len(design) * i + t] = tile
    per = material_ref.shape[1] // 8
    spot = per * n
    for ref in (free_ref, rhs_ref):
        for i in range(2, n):
            for tile in tiles_of(ref, i):
                x_up_ref[spot] = tile
                spot += 1
    spot = per * n
    for ref, count in ((free_ref, n - 1), (rhs_ref, n - 1), (warmth_ref, 1)):
        for i in range(count):
            for tile in tiles_of(ref, i):
                x_down_ref[spot] = tile
                spot += 1


def corner_kernel(n, low_ref, high_ref, up_ref, down_ref):
    half = up_ref.shape[0] // 2
    up_ref[:n] = low_ref[:n]
    up_ref[n:half] = low_ref[n + 2 :]
    up_ref[half : half + n] = high_ref[:n]
    up_ref[half + n :] = high_ref[n + 2 :]
    half = down_ref.shape[0] // 2
    down_ref[:n] = low_ref[:n]
    down_ref[n:half] = low_ref[n : 2 * n - 1]
    down_ref[half : half + n] = high_ref[:n]
    down_ref[half + n :] = high_ref[n : 2 * n - 1]


def brick(n, own_rows, own, y_low, y_high, x_low, x_high, corner_low, corner_high):
    design_ref, free_ref, rhs_ref, warmth_ref = own
    per = own_rows // 8

    def rows_of(ref, start):
        return ref[start : start + per].reshape(own_rows, ref.shape[-1])

    def own_part(which, i):
        if 0 <= i < n:
            return own[which][i]
        if i < 0:
            return rows_of(x_low, per * ((i + n) if which == 0 else n + (which - 1) * (n - 2) + i + n - 2))
        return rows_of(x_high, per * ((i - n) if which == 0 else n + (which - 1) * (n - 1) + i - n))

    def y_tile(first, high, i):
        if 0 <= i < n:
            return (y_high if high else y_low)[i if first else n + i]
        ref, at, count = (corner_low, i + n, n - 2) if i < 0 else (corner_high, i - n, n - 1)
        start = (n + count) if high else 0
        if first:
            return ref[start + at]
        return ref[start + n + (i + n - 2 if i < 0 else at)]

    def joined(low, middle, high):
        return jnp.concatenate([low, middle, high], axis=0)

    def near(value):
        return value[WIDE - NEAR : own_rows + WIDE + NEAR]

    def design_at(i):
        return joined(y_tile(True, False, i), own_part(0, i), y_tile(True, True, i))

    def free_at(i):
        return near(
            joined(roll_rows(y_tile(True, False, i), -3), own_part(1, i), roll_rows(y_tile(False, True, i), -4))
        )

    def rhs_at(i):
        return near(joined(y_tile(False, False, i), own_part(2, i), y_tile(False, True, i)))

    def warmth_at(i):
        return near(
            joined(roll_rows(y_tile(False, False, i), -1), own_part(3, i), roll_rows(y_tile(True, True, i), -5))
        )

    return design_at, free_at, rhs_at, warmth_at


def basis_kernel(
    n, own_rows, layers, rows,
    design_ref, free_ref, rhs_ref, y_low, y_high, x_low, x_high, corner_low, corner_high,
    moments_ref, basis_ref, solid_ref,
    conduct_s, free_s, diag_inverse_s, u0_s, u1_s,
):
    first_layer = lax.axis_index("gx") * n
    first_row = lax.axis_index("gy") * own_rows
    wide_rows = own_rows + 2 * WIDE
    near_rows = own_rows + 2 * NEAR
    z = design_ref.shape[-1]
    design_at, free_from, rhs_at, _ = brick(
        n, own_rows, (design_ref, free_ref, rhs_ref, None),
        y_low, y_high, x_low, x_high, corner_low, corner_high,
    )

    for i in range(1 - n, 2 * n - 1):
        valid, weight = filter_weight(i, layers, first_layer, first_row - WIDE, rows, (wide_rows, z))
        solid = 1.0 - filtered(design_at(i - 1), design_at(i), design_at(i + 1)) / weight
        solid = solid[WIDE - NEAR : wide_rows - WIDE + NEAR]
        valid = valid[WIDE - NEAR : wide_rows - WIDE + NEAR]
        conduct_s[i + n - 1] = jnp.where(valid > 0, KMIN + (1.0 - KMIN) * (solid * solid * solid), 0.0)
        if 0 <= i < n:
            solid_ref[i] = solid

    def conduct_at(i):
        return conduct_s[i + n - 1]

    def free_at(i):
        return free_s[i + n - 2]

    for i in range(2 - n, 2 * n - 1):
        pair = conduct_at(i) + conduct_at(i - 1)
        pair = pair + down(pair, 0)
        pair = pair + lower_z(pair)
        free = free_from(i)
        inverse = 1.0 / (free * (pair * (1.0 / 3.0)) + (1.0 - free))
        free_s[i + n - 2] = free
        diag_inverse_s[i + n - 2] = inverse
        u0_s[i + n - 2] = rhs_at(i) * inverse

    row = lax.broadcasted_iota(jnp.int32, (near_rows, z), 0)
    own = (row >= NEAR) & (row < NEAR + own_rows)
    sums = [jnp.zeros((8, 128), jnp.float32) for _ in range(MOMENTS)]

    def gather(which, product):
        sums[which] = sums[which] + tile_sum(jnp.where(own, product, 0.0))

    def step(previous, first, count):
        for i, image in apply_layers(lambda i: free_at(i) * previous(i), conduct_at, first, count):
            free, start = free_at(i), previous(i)
            image = free * image + (1.0 - free) * start
            yield i, start, image, image * diag_inverse_s[i + n - 2] - start

    for i, start, image, later in step(lambda i: u0_s[i + n - 2], 3 - n, 3 * n - 5):
        u1_s[i + n - 3] = later
        if 0 <= i <= n:
            basis_ref[0, i] = start
        if 0 <= i < n:
            rhs = rhs_at(i)
            gather(0, start * image)
            gather(1, later * image)
            gather(5, rhs * start)
            gather(6, rhs * later)
    for i, start, image, later in step(lambda i: u1_s[i + n - 3], 0, n + 1):
        basis_ref[1, i] = start
        basis_ref[2, i] = later
        if i < n:
            gather(2, start * image)
            gather(3, later * image)
            gather(7, rhs_at(i) * later)
    low = yz_modes(free_at(0) * basis_ref[2, 0])
    for i in range(n):
        high = yz_modes(free_at(i + 1) * basis_ref[2, i + 1])
        square = sum(order * value * value for order, value in element_modes(low, high).values())
        last = basis_ref[2, i]
        gather(4, square * (conduct_at(i) * (1.0 / 48.0)) + (1.0 - free_at(i)) * last * last)
        low = high

    lane = lax.broadcasted_iota(jnp.int32, (1, 128), 1)
    total = jnp.zeros((1, 128), jnp.float32)
    for k in range(MOMENTS):
        total = total + jnp.where(lane == k, jnp.sum(sums[k], axis=(0, 1), keepdims=True), 0.0)
    moments_ref[...] = jnp.broadcast_to(total, moments_ref.shape)


def integrand_kernel(
    n, own_rows, layers, rows,
    basis_ref, solid_ref, warmth_ref, y_low, y_high, x_low, x_high, corner_low, corner_high,
    scaled_ref, first_ref, last_ref,
):
    first_layer = lax.axis_index("gx") * n
    first_row = lax.axis_index("gy") * own_rows
    shape = solid_ref.shape[1:]
    *_, warmth_at = brick(
        n, own_rows, (None, None, None, warmth_ref),
        y_low, y_high, x_low, x_high, corner_low, corner_high,
    )
    warm_low = yz_modes(warmth_at(0))
    lows = [yz_modes(basis_ref[k, 0]) for k in range(BASIS)]
    for i in range(n):
        warm_high = yz_modes(warmth_at(i + 1))
        valid, weight = filter_weight(i, layers, first_layer, first_row - NEAR, rows, shape)
        solid = solid_ref[i]
        share = jnp.where(valid > 0, 3.0 * solid * solid / weight, 0.0)
        load = {
            key: (order / 48.0) * value for key, (order, value) in element_modes(warm_low, warm_high).items()
        }
        for k in range(BASIS):
            high = yz_modes(basis_ref[k, i + 1])
            modes = element_modes(lows[k], high)
            energy = sum(load[key] * value for key, (_, value) in modes.items())
            total = lows[k][0] + high[0]
            result = share * ((1.0 - KMIN) * energy - (QZERO / 8.0) * total)
            scaled_ref[k, i] = result
            if i == 0:
                first_ref[k] = result
            if i == n - 1:
                last_ref[k] = result
            lows[k] = high
        warm_low = warm_high


def filter_kernel(n, own_rows, scaled_ref, below_ref, above_ref, parts_ref):
    for k in range(BASIS):
        for i in range(n):
            below = scaled_ref[k, i - 1] if i > 0 else below_ref[k]
            above = scaled_ref[k, i + 1] if i < n - 1 else above_ref[k]
            parts_ref[k, i] = filtered(below, scaled_ref[k, i], above)[NEAR : NEAR + own_rows]


def final_kernel(n, own_rows, moments_ref, basis_ref, parts_ref, dual_ref, sens_ref):
    total = jnp.sum(moments_ref[...], axis=0, keepdims=True)
    a0, a1, a2, a3, a4, b0, b1, b2 = (
        jnp.broadcast_to(total[:, k : k + 1], (1, 128)) for k in range(MOMENTS)
    )
    l10 = a1 / a0
    l20 = a2 / a0
    d1 = a2 - l10 * a1
    t21 = a3 - l20 * a1
    l21 = t21 / d1
    d2 = a4 - l20 * a2 - l21 * t21
    z1 = b1 - l10 * b0
    z2 = b2 - l20 * b0 - l21 * z1
    y2 = z2 / d2
    y1 = z1 / d1 - l21 * y2
    y0 = b0 / a0 - l10 * y1 - l20 * y2
    z = dual_ref.shape[-1]
    coefs = [jnp.concatenate([y] * (z // 128), axis=1) for y in (y0, y1, y2)]
    for i in range(n):
        dual = sum(coefs[k] * basis_ref[k, i] for k in range(BASIS))
        dual_ref[i] = dual[NEAR : NEAR + own_rows]
        sens_ref[i] = sum(coefs[k] * parts_ref[k, i] for k in range(BASIS))


def shifted(arr, axis, step):
    count = lax.axis_size(axis)
    return lax.ppermute(arr, axis, [(i, i + step) for i in range(count) if 0 <= i + step < count])


def in_vmem(count):
    return [pl.BlockSpec(memory_space=pltpu.VMEM)] * count


def body(gx, gy, material_fraction, primal_warmth, empty_region_flags, dirichlet_flags):
    n, own_rows, z = material_fraction.shape
    sizes = (n, own_rows, gx * n, gy * own_rows)
    near = own_rows + 2 * NEAR
    per = own_rows // 8

    def arrays(*shapes):
        return [jax.ShapeDtypeStruct(shape, jnp.float32) for shape in shapes]

    def call(name, kernel, outs, *operands, scratch=(), resident=True, flops=0):
        return pl.pallas_call(
            kernel,
            out_shape=arrays(*outs),
            in_specs=in_vmem(len(operands)) if resident else None,
            out_specs=in_vmem(len(outs)) if resident else None,
            scratch_shapes=[pltpu.VMEM(shape, jnp.float32) for shape in scratch],
            compiler_params=pltpu.CompilerParams(vmem_limit_bytes=VMEM_LIMIT),
            cost_estimate=pl.CostEstimate(flops=flops, bytes_accessed=1 << 20, transcendentals=0),
            name=name,
        )(*operands)

    brick_shape = (n, own_rows, z)
    free, rhs, warmth, y_up, y_down, x_up, x_down = call(
        "pack",
        functools.partial(pack_kernel, n),
        [brick_shape] * 3
        + [(2 * n, 8, z)] * 2
        + [(per * (n + 2 * (n - 2)), 8, z), (per * (n + 2 * (n - 1) + 1), 8, z)],
        material_fraction, primal_warmth, empty_region_flags, dirichlet_flags,
    )
    y_low = shifted(y_up, "gy", 1)
    y_high = shifted(y_down, "gy", -1)
    x_low = shifted(x_up, "gx", 1)
    x_high = shifted(x_down, "gx", -1)
    corner_up, corner_down = call(
        "corners",
        functools.partial(corner_kernel, n),
        [(2 * (2 * n - 2), 8, z), (2 * (2 * n - 1), 8, z)],
        y_low, y_high,
    )
    corner_low = shifted(corner_up, "gx", 1)
    corner_high = shifted(corner_down, "gx", -1)
    halo = (y_low, y_high, x_low, x_high, corner_low, corner_high)

    pairs = 2 if gx % 2 == 0 else 1
    inner, outer = pairs * gy, gx // pairs
    moments, basis, solid = call(
        "basis",
        functools.partial(basis_kernel, *sizes),
        [(inner, 128), (BASIS, n + 1, near, z), (n, near, z)],
        material_fraction, free, rhs, *halo,
        scratch=[
            (3 * n - 2, near, z),
            (3 * n - 3, near, z),
            (3 * n - 3, near, z),
            (3 * n - 3, near, z),
            (3 * n - 5, near, z),
        ],
    )
    scaled, first, last = call(
        "integrand",
        functools.partial(integrand_kernel, *sizes),
        [(BASIS, n, near, z), (BASIS, near, z), (BASIS, near, z)],
        basis, solid, warmth, *halo,
        flops=40000000,
    )
    near_groups = [
        [(g * pairs + c) * gy + y for c in range(pairs) for y in range(gy)] for g in range(outer)
    ]
    far_groups = [
        [(g * pairs + c) * gy + y for g in range(outer)] for c in range(pairs) for y in range(gy)
    ]
    moments = lax.all_to_all(moments, ("gx", "gy"), 0, 0, axis_index_groups=near_groups, tiled=True)
    near_total = jnp.sum(moments, axis=0, keepdims=True)
    near_total, first, last = lax.optimization_barrier((near_total, first, last))
    moments = jnp.broadcast_to(near_total, (outer, 128))
    below = shifted(last, "gx", 1)
    above = shifted(first, "gx", -1)
    (parts,) = call(
        "filter",
        functools.partial(filter_kernel, n, own_rows),
        [(BASIS,) + brick_shape],
        scaled, below, above,
        flops=1000000,
    )
    moments = lax.all_to_all(moments, ("gx", "gy"), 0, 0, axis_index_groups=far_groups, tiled=True)
    return tuple(
        call(
            "combine",
            functools.partial(final_kernel, n, own_rows),
            [brick_shape, brick_shape],
            moments, basis, parts,
        )
    )


def solution(mesh):
    placed = P("gx", "gy", None)
    return jax.shard_map(
        functools.partial(body, mesh.shape["gx"], mesh.shape["gy"]),
        mesh=mesh,
        in_specs=(placed,) * 4,
        out_specs=(placed, placed),
        check_vma=False,
    )
```

```python
import functools
import math

import jax
import jax.numpy as jnp
from jax import lax
from jax.experimental import pallas as pl
from jax.experimental.pallas import tpu as pltpu
from jax.sharding import PartitionSpec as P

KMIN = 0.05
QZERO = 1.0
EDGE = 0.5
DIAGONAL = 1.5 - math.sqrt(2.0)

WIDE = 8
NEAR = 4
BASIS = 3
MOMENTS = 8
VMEM_LIMIT = 12 << 20
LOAD_LIMIT = 857 << 16


def up(arr, axis):
    return pltpu.roll(arr, arr.shape[axis] - 1, axis)


def down(arr, axis):
    return pltpu.roll(arr, 1, axis)


def z_index(arr):
    return lax.broadcasted_iota(jnp.int32, arr.shape, 1)


def lift(arr):
    return jnp.where(z_index(arr) == arr.shape[1] - 1, 0.0, up(arr, 1))


def lower_z(arr):
    return jnp.where(z_index(arr) == 0, 0.0, down(arr, 1))


def filtered(below, here, above):
    beside = below + above
    rim = up(here, 0) + down(here, 0)
    corner = up(beside, 0) + down(beside, 0)
    flat = 1.5 * here + EDGE * (beside + rim) + DIAGONAL * corner
    slanted = EDGE * here + DIAGONAL * (beside + rim)
    return flat + lift(slanted) + lower_z(slanted)


def grid_flags(layer, layers, first_layer, first_row, rows, shape):
    def inside(at):
        return ((at >= 0) & (at < layers)).astype(jnp.float32)

    at = first_layer + layer
    row = first_row + lax.broadcasted_iota(jnp.int32, shape, 0)

    def row_inside(offset):
        return ((row + offset >= 0) & (row + offset < rows)).astype(jnp.float32)

    return inside(at), inside(at - 1) + inside(at + 1), row_inside(0), row_inside(-1) + row_inside(1)


def filter_weight(layer, layers, first_layer, first_row, rows, shape):
    here, beside, row_here, row_beside = grid_flags(
        layer, layers, first_layer, first_row, rows, shape
    )
    z = lax.broadcasted_iota(jnp.int32, shape, 1)
    z_beside = (z > 0).astype(jnp.float32) + (z < shape[1] - 1).astype(jnp.float32)
    flat = (1.5 + EDGE * beside) * row_here + (EDGE + DIAGONAL * beside) * row_beside
    slanted = (EDGE + DIAGONAL * beside) * row_here + DIAGONAL * row_beside
    valid = here * row_here
    return valid, jnp.where(valid > 0, flat + z_beside * slanted, 1.0)


def yz_modes(node):
    lifted = lift(node)
    plain, slope = node + lifted, lifted - node
    plain_up, slope_up = up(plain, 0), up(slope, 0)
    return plain + plain_up, slope + slope_up, plain_up - plain, slope_up - slope


def element_modes(low, high):
    return {
        "d0": (3.0, high[0] - low[0]),
        "s1": (3.0, high[1] + low[1]),
        "s2": (3.0, high[2] + low[2]),
        "d1": (2.0, high[1] - low[1]),
        "d2": (2.0, high[2] - low[2]),
        "s3": (2.0, high[3] + low[3]),
        "d3": (1.0, high[3] - low[3]),
    }


def apply_layers(node_at, conduct_at, first, count):
    low = yz_modes(node_at(first - 1))
    carried = None
    for element in range(first - 1, first + count):
        high = yz_modes(node_at(element + 1))
        scaled = conduct_at(element) * (1.0 / 48.0)
        flow = {key: (order * value) * scaled for key, (order, value) in element_modes(low, high).items()}
        zero_sum = flow["d0"]
        if carried is not None:
            planes = (
                carried[0] - zero_sum,
                carried[1] + (flow["s1"] - flow["d1"]),
                carried[2] + (flow["s2"] - flow["d2"]),
                carried[3] + (flow["s3"] - flow["d3"]),
            )
            smooth = (planes[0] - planes[2]) + down(planes[0] + planes[2], 0)
            slope = (planes[1] - planes[3]) + down(planes[1] + planes[3], 0)
            yield element, (smooth - slope) + lower_z(smooth + slope)
        carried = (
            zero_sum,
            flow["s1"] + flow["d1"],
            flow["s2"] + flow["d2"],
            flow["s3"] + flow["d3"],
        )
        low = high


def tile_sum(value):
    return functools.reduce(
        jnp.add,
        [
            value[r : r + 8, c : c + 128]
            for r in range(0, value.shape[0], 8)
            for c in range(0, value.shape[1], 128)
        ],
    )


def roll_rows(tile, step):
    return pltpu.roll(tile, step % tile.shape[0], 0)


def load_kernel(
    n, material_hbm, primal_hbm, source_hbm, fixed_hbm,
    design_ref, free_ref, rhs_ref, warmth_ref, y_up_ref, y_down_ref,
    primal_ref, source_ref, fixed_ref, arrived,
):
    copies = [
        pltpu.make_async_copy(source, target, arrived.at[k])
        for k, (source, target) in enumerate(
            (
                (material_hbm, design_ref),
                (primal_hbm, primal_ref),
                (source_hbm, source_ref),
                (fixed_hbm, fixed_ref),
            )
        )
    ]
    for copy in copies:
        copy.start()
    for copy in copies:
        copy.wait()
    row = lax.broadcasted_iota(jnp.int32, (8, design_ref.shape[-1]), 0)
    for i in range(n):
        free = (1 - fixed_ref[i]).astype(jnp.float32)
        warmth = free * primal_ref[i]
        rhs = source_ref[i].astype(jnp.float32) * warmth
        design = design_ref[i]
        free_ref[i] = free
        warmth_ref[i] = warmth
        rhs_ref[i] = rhs
        y_up_ref[i] = jnp.where(row >= 3, design[-8:], roll_rows(free[-8:], 3))
        y_up_ref[n + i] = jnp.where(row >= 5, rhs[-8:], roll_rows(warmth[-8:], 1))
        y_down_ref[i] = jnp.where(row < 5, design[:8], roll_rows(warmth[:8], 5))
        y_down_ref[n + i] = jnp.where(row < 4, rhs[:8], roll_rows(free[:8], 4))


def extend_kernel(
    n, own_rows, design_in, free_in, rhs_in, warmth_in, low_ref, high_ref,
    design_ref, free_ref, rhs_ref, warmth_ref, up_ref, down_ref, far_up_ref, far_down_ref,
):
    z = design_in.shape[-1]

    def joined(low, middle, high):
        return jnp.concatenate([low, middle, high], axis=0)

    def near(low, middle, high):
        return joined(low, middle, high)[WIDE - NEAR : own_rows + WIDE + NEAR]

    spots = {id(up_ref): 0, id(down_ref): 0}

    def put(ref, value):
        count = value.shape[0] // 8
        spot = spots[id(ref)]
        ref[spot : spot + count] = value.reshape(count, 8, z)
        spots[id(ref)] = spot + count

    for i in range(n):
        value = joined(low_ref[i], design_in[i], high_ref[i])
        design_ref[i] = value
        put(up_ref, value)
        put(down_ref, value)
        if i == 0:
            far_down_ref[0] = value
        if i == n - 1:
            far_up_ref[0] = value
    for i in range(n):
        value = near(roll_rows(low_ref[i], -3), free_in[i], roll_rows(high_ref[n + i], -4))
        free_ref[i] = value
        put(down_ref, value)
        if i > 0:
            put(up_ref, value)
    for i in range(n):
        value = near(low_ref[n + i], rhs_in[i], high_ref[n + i])
        rhs_ref[i] = value
        put(down_ref, value)
        if i > 0:
            put(up_ref, value)
    for i in range(n):
        value = near(roll_rows(low_ref[n + i], -1), warmth_in[i], roll_rows(high_ref[i], -5))
        warmth_ref[i] = value
        if i < 2:
            put(down_ref, value)
        if i == n - 1:
            put(up_ref, value)


def basis_kernel(
    n, own_rows, layers, rows,
    design_ref, free_ref, rhs_ref, lo_ref, hi_ref, below_ref, above_ref,
    moments_ref, basis_ref, solid_ref,
    conduct_s, inv_s, u0_s, u1_s,
):
    first_layer = lax.axis_index("gx") * n
    first_row = lax.axis_index("gy") * own_rows
    wide_rows = own_rows + 2 * WIDE
    near_rows = own_rows + 2 * NEAR
    wide_tiles, near_tiles = wide_rows // 8, near_rows // 8
    z = design_ref.shape[-1]

    def design_at(i):
        if i == -n - 1:
            return below_ref[0]
        if i == 2 * n:
            return above_ref[0]
        if 0 <= i < n:
            return design_ref[i]
        ref, at = (lo_ref, i + n) if i < 0 else (hi_ref, i - n)
        return ref[at * wide_tiles : (at + 1) * wide_tiles].reshape(wide_rows, z)

    def node_at(which, own_ref):
        def at(i):
            if 0 <= i < n:
                return own_ref[i]
            if i < 0:
                start = n * wide_tiles + (which * (n - 1) + i + n - 1) * near_tiles
                return lo_ref[start : start + near_tiles].reshape(near_rows, z)
            start = n * wide_tiles + (which * n + i - n) * near_tiles
            return hi_ref[start : start + near_tiles].reshape(near_rows, z)

        return at

    free_at, rhs_at = node_at(0, free_ref), node_at(1, rhs_ref)

    for i in range(-n, 2 * n):
        valid, weight = filter_weight(i, layers, first_layer, first_row - WIDE, rows, (wide_rows, z))
        solid = 1.0 - filtered(design_at(i - 1), design_at(i), design_at(i + 1)) / weight
        solid = solid[WIDE - NEAR : wide_rows - WIDE + NEAR]
        valid = valid[WIDE - NEAR : wide_rows - WIDE + NEAR]
        conduct_s[i + n] = jnp.where(valid > 0, KMIN + (1.0 - KMIN) * (solid * solid * solid), 0.0)
        if -1 <= i <= n:
            solid_ref[i + 1] = solid

    for i in range(1 - n, 2 * n):
        pair = conduct_s[i + n] + conduct_s[i + n - 1]
        pair = pair + down(pair, 0)
        pair = pair + lower_z(pair)
        free = free_at(i)
        diag = free * (pair * (1.0 / 3.0)) + (1.0 - free)
        inverse = 1.0 / diag
        inv_s[i + n - 1] = inverse
        u0_s[i + n - 1] = rhs_at(i) * inverse

    row = lax.broadcasted_iota(jnp.int32, (near_rows, z), 0)
    own = (row >= NEAR) & (row < NEAR + own_rows)
    sums = [jnp.zeros((8, 128), jnp.float32) for _ in range(MOMENTS)]

    def gather(which, product):
        sums[which] = sums[which] + tile_sum(jnp.where(own, product, 0.0))

    def conduct_at(i):
        return conduct_s[i + n]

    for i, image in apply_layers(
        lambda i: free_at(i) * u0_s[i + n - 1], conduct_at, 2 - n, 3 * n - 3
    ):
        free, start = free_at(i), u0_s[i + n - 1]
        image = free * image + (1.0 - free) * start
        later = image * inv_s[i + n - 1] - start
        u1_s[i + n - 2] = later
        if -1 <= i <= n + 1:
            basis_ref[0, i + 1] = start
        if 0 <= i < n:
            gather(0, start * image)
            gather(1, later * image)
            gather(5, rhs_at(i) * start)
            gather(6, rhs_at(i) * later)
    for i, image in apply_layers(
        lambda i: free_at(i) * u1_s[i + n - 2], conduct_at, -1, n + 3
    ):
        free, start = free_at(i), u1_s[i + n - 2]
        image = free * image + (1.0 - free) * start
        later = image * inv_s[i + n - 1] - start
        basis_ref[1, i + 1] = start
        basis_ref[2, i + 1] = later
        if 0 <= i < n:
            gather(2, start * image)
            gather(3, later * image)
            gather(7, rhs_at(i) * later)
    low = yz_modes(free_at(0) * basis_ref[2, 1])
    for i in range(n):
        high = yz_modes(free_at(i + 1) * basis_ref[2, i + 2])
        square = sum(order * value * value for order, value in element_modes(low, high).values())
        last = basis_ref[2, i + 1]
        gather(4, square * (conduct_at(i) * (1.0 / 48.0)) + (1.0 - free_at(i)) * last * last)
        low = high

    lane = lax.broadcasted_iota(jnp.int32, (1, 128), 1)
    total = jnp.zeros((1, 128), jnp.float32)
    for k in range(MOMENTS):
        total = total + jnp.where(lane == k, jnp.sum(sums[k], axis=(0, 1), keepdims=True), 0.0)
    moments_ref[...] = jnp.broadcast_to(total, moments_ref.shape)


def sensitivity_kernel(
    n, own_rows, layers, rows,
    basis_ref, solid_ref, warmth_ref, lo_ref, hi_ref,
    parts_ref,
    scaled_s,
):
    first_layer = lax.axis_index("gx") * n
    first_row = lax.axis_index("gy") * own_rows
    near_rows = own_rows + 2 * NEAR
    near_tiles = near_rows // 8
    z = solid_ref.shape[-1]
    shape = (near_rows, z)

    def warmth_at(i):
        if 0 <= i < n:
            return warmth_ref[i]
        if i < 0:
            return lo_ref[lo_ref.shape[0] - near_tiles :].reshape(shape)
        start = hi_ref.shape[0] - (n + 2 - i) * near_tiles
        return hi_ref[start : start + near_tiles].reshape(shape)

    warm_low = yz_modes(warmth_at(-1))
    lows = [yz_modes(basis_ref[k, 0]) for k in range(BASIS)]
    for i in range(-1, n + 1):
        warm_high = yz_modes(warmth_at(i + 1))
        valid, weight = filter_weight(i, layers, first_layer, first_row - NEAR, rows, shape)
        solid = solid_ref[i + 1]
        share = jnp.where(valid > 0, 3.0 * solid * solid / weight, 0.0)
        load = {
            key: (order / 48.0) * value for key, (order, value) in element_modes(warm_low, warm_high).items()
        }
        for k in range(BASIS):
            high = yz_modes(basis_ref[k, i + 2])
            modes = element_modes(lows[k], high)
            energy = sum(load[key] * value for key, (_, value) in modes.items())
            total = lows[k][0] + high[0]
            scaled_s[k, i + 1] = share * ((1.0 - KMIN) * energy - (QZERO / 8.0) * total)
            lows[k] = high
        warm_low = warm_high
    for k in range(BASIS):
        for i in range(n):
            result = filtered(scaled_s[k, i], scaled_s[k, i + 1], scaled_s[k, i + 2])
            parts_ref[k, i] = result[NEAR : NEAR + own_rows]


def final_kernel(n, own_rows, moments_ref, basis_ref, parts_ref, dual_ref, sens_ref):
    total = jnp.sum(moments_ref[...], axis=0, keepdims=True)
    a0, a1, a2, a3, a4, b0, b1, b2 = (
        jnp.broadcast_to(total[:, k : k + 1], (1, 128)) for k in range(MOMENTS)
    )
    l10 = a1 / a0
    l20 = a2 / a0
    d1 = a2 - l10 * a1
    t21 = a3 - l20 * a1
    l21 = t21 / d1
    d2 = a4 - l20 * a2 - l21 * t21
    z1 = b1 - l10 * b0
    z2 = b2 - l20 * b0 - l21 * z1
    y2 = z2 / d2
    y1 = z1 / d1 - l21 * y2
    y0 = b0 / a0 - l10 * y1 - l20 * y2
    z = dual_ref.shape[-1]
    coefs = [jnp.concatenate([y] * (z // 128), axis=1) for y in (y0, y1, y2)]
    for i in range(n):
        dual = sum(coefs[k] * basis_ref[k, i + 1] for k in range(BASIS))
        dual_ref[i] = dual[NEAR : NEAR + own_rows]
        sens_ref[i] = sum(coefs[k] * parts_ref[k, i] for k in range(BASIS))


def shifted(arr, axis, step):
    count = lax.axis_size(axis)
    return lax.ppermute(arr, axis, [(i, i + step) for i in range(count) if 0 <= i + step < count])


def body(gx, gy, material_fraction, primal_warmth, empty_region_flags, dirichlet_flags):
    n, own_rows, z = material_fraction.shape
    sizes = (n, own_rows, gx * n, gy * own_rows)
    near, wide = own_rows + 2 * NEAR, own_rows + 2 * WIDE
    near_tiles, wide_tiles = near // 8, wide // 8

    def call(name, kernel, outs, *operands, scratch=(), space=pltpu.VMEM, limit=VMEM_LIMIT, flops=0):
        return pl.pallas_call(
            kernel,
            out_shape=[jax.ShapeDtypeStruct(shape, jnp.float32) for shape in outs],
            in_specs=[pl.BlockSpec(memory_space=space)] * len(operands),
            out_specs=[pl.BlockSpec(memory_space=pltpu.VMEM)] * len(outs),
            scratch_shapes=list(scratch),
            compiler_params=pltpu.CompilerParams(vmem_limit_bytes=limit),
            cost_estimate=pl.CostEstimate(flops=flops, bytes_accessed=1 << 20, transcendentals=0),
            name=name,
        )(*operands)

    def floats(*shape):
        return pltpu.VMEM(shape, jnp.float32)

    brick_shape = (n, own_rows, z)
    *own, y_up, y_down = call(
        "load",
        functools.partial(load_kernel, n),
        [brick_shape] * 4 + [(2 * n, 8, z)] * 2,
        material_fraction, primal_warmth, empty_region_flags, dirichlet_flags,
        scratch=[
            floats(*brick_shape),
            pltpu.VMEM(brick_shape, jnp.int32),
            pltpu.VMEM(brick_shape, jnp.int32),
            pltpu.SemaphoreType.DMA((4,)),
        ],
        space=pltpu.HBM,
        limit=LOAD_LIMIT,
    )
    y_low = shifted(y_up, "gy", 1)
    y_high = shifted(y_down, "gy", -1)
    up_tiles = n * wide_tiles + (2 * (n - 1) + 1) * near_tiles
    down_tiles = n * wide_tiles + (2 * n + 2) * near_tiles
    design, free, rhs, warmth, up, down, far_up, far_down = call(
        "extend",
        functools.partial(extend_kernel, n, own_rows),
        [(n, wide, z)] + [(n, near, z)] * 3
        + [(up_tiles, 8, z), (down_tiles, 8, z), (1, wide, z), (1, wide, z)],
        *own, y_low, y_high,
    )
    lo = shifted(up, "gx", 1)
    hi = shifted(down, "gx", -1)
    below = shifted(far_up, "gx", 2)
    above = shifted(far_down, "gx", -2)

    inner = min(16, gx)
    outer = gx * gy // inner
    moments, basis, solid = call(
        "basis",
        functools.partial(basis_kernel, *sizes),
        [(inner, 128), (BASIS, n + 3, near, z), (n + 2, near, z)],
        design, free, rhs, lo, hi, below, above,
        scratch=[
            floats(3 * n, near, z),
            floats(3 * n - 1, near, z),
            floats(3 * n - 1, near, z),
            floats(3 * n - 3, near, z),
        ],
    )
    (parts,) = call(
        "sensitivity_parts",
        functools.partial(sensitivity_kernel, *sizes),
        [(BASIS,) + brick_shape],
        basis, solid, warmth, lo, hi,
        scratch=[floats(BASIS, n + 2, near, z)],
        flops=40000000,
    )

    first = [[g * inner + j for j in range(inner)] for g in range(gx // inner)]
    first = [[d * gy + y for d in group] for group in first for y in range(gy)]
    second = [
        [(g * inner + j) * gy + y for g in range(gx // inner) for y in range(gy)]
        for j in range(inner)
    ]
    moments = lax.all_to_all(moments, ("gx", "gy"), 0, 0, axis_index_groups=first, tiled=True)
    moments = jnp.broadcast_to(jnp.sum(moments, axis=0, keepdims=True), (outer, 128))
    moments = lax.all_to_all(moments, ("gx", "gy"), 0, 0, axis_index_groups=second, tiled=True)
    return tuple(
        call(
            "combine",
            functools.partial(final_kernel, n, own_rows),
            [brick_shape, brick_shape],
            moments, basis, parts,
        )
    )


def solution(mesh):
    placed = P("gx", "gy", None)
    return jax.shard_map(
        functools.partial(body, mesh.shape["gx"], mesh.shape["gy"]),
        mesh=mesh,
        in_specs=(placed,) * 4,
        out_specs=(placed, placed),
        check_vma=False,
    )
```

```python
import functools
import math

import jax
import jax.numpy as jnp
from jax import lax
from jax.experimental import pallas as pl
from jax.experimental.pallas import tpu as pltpu
from jax.sharding import PartitionSpec as P

KMIN = 0.05
QZERO = 1.0
EDGE = 0.5
DIAGONAL = 1.5 - math.sqrt(2.0)

WIDE = 8
NEAR = 4
BASIS = 3
MOMENTS = 8
VMEM_LIMIT = 12 << 20
FAR_WORK = 10**10
LOAD_LIMIT = 857 << 16


def up(arr, axis):
    return pltpu.roll(arr, arr.shape[axis] - 1, axis)


def down(arr, axis):
    return pltpu.roll(arr, 1, axis)


def z_index(arr):
    return lax.broadcasted_iota(jnp.int32, arr.shape, 1)


def lift(arr):
    return jnp.where(z_index(arr) == arr.shape[1] - 1, 0.0, up(arr, 1))


def lower_z(arr):
    return jnp.where(z_index(arr) == 0, 0.0, down(arr, 1))


def filtered(below, here, above):
    beside = below + above
    rim = up(here, 0) + down(here, 0)
    corner = up(beside, 0) + down(beside, 0)
    flat = 1.5 * here + EDGE * (beside + rim) + DIAGONAL * corner
    slanted = EDGE * here + DIAGONAL * (beside + rim)
    return flat + lift(slanted) + lower_z(slanted)


def grid_flags(layer, layers, first_layer, first_row, rows, shape):
    def inside(at):
        return ((at >= 0) & (at < layers)).astype(jnp.float32)

    at = first_layer + layer
    row = first_row + lax.broadcasted_iota(jnp.int32, shape, 0)

    def row_inside(offset):
        return ((row + offset >= 0) & (row + offset < rows)).astype(jnp.float32)

    return inside(at), inside(at - 1) + inside(at + 1), row_inside(0), row_inside(-1) + row_inside(1)


def filter_weight(layer, layers, first_layer, first_row, rows, shape):
    here, beside, row_here, row_beside = grid_flags(
        layer, layers, first_layer, first_row, rows, shape
    )
    z = lax.broadcasted_iota(jnp.int32, shape, 1)
    z_beside = (z > 0).astype(jnp.float32) + (z < shape[1] - 1).astype(jnp.float32)
    flat = (1.5 + EDGE * beside) * row_here + (EDGE + DIAGONAL * beside) * row_beside
    slanted = (EDGE + DIAGONAL * beside) * row_here + DIAGONAL * row_beside
    valid = here * row_here
    return valid, jnp.where(valid > 0, flat + z_beside * slanted, 1.0)


def yz_modes(node):
    lifted = lift(node)
    plain, slope = node + lifted, lifted - node
    plain_up, slope_up = up(plain, 0), up(slope, 0)
    return plain + plain_up, slope + slope_up, plain_up - plain, slope_up - slope


def element_modes(low, high):
    return {
        "d0": (3.0, high[0] - low[0]),
        "s1": (3.0, high[1] + low[1]),
        "s2": (3.0, high[2] + low[2]),
        "d1": (2.0, high[1] - low[1]),
        "d2": (2.0, high[2] - low[2]),
        "s3": (2.0, high[3] + low[3]),
        "d3": (1.0, high[3] - low[3]),
    }


def apply_layers(node_at, conduct_at, first, count):
    low = yz_modes(node_at(first - 1))
    carried = None
    for element in range(first - 1, first + count):
        high = yz_modes(node_at(element + 1))
        scaled = conduct_at(element) * (1.0 / 48.0)
        flow = {key: (order * value) * scaled for key, (order, value) in element_modes(low, high).items()}
        zero_sum = flow["d0"]
        if carried is not None:
            planes = (
                carried[0] - zero_sum,
                carried[1] + (flow["s1"] - flow["d1"]),
                carried[2] + (flow["s2"] - flow["d2"]),
                carried[3] + (flow["s3"] - flow["d3"]),
            )
            smooth = (planes[0] - planes[2]) + down(planes[0] + planes[2], 0)
            slope = (planes[1] - planes[3]) + down(planes[1] + planes[3], 0)
            yield element, (smooth - slope) + lower_z(smooth + slope)
        carried = (
            zero_sum,
            flow["s1"] + flow["d1"],
            flow["s2"] + flow["d2"],
            flow["s3"] + flow["d3"],
        )
        low = high


def tile_sum(value):
    return functools.reduce(
        jnp.add,
        [
            value[r : r + 8, c : c + 128]
            for r in range(0, value.shape[0], 8)
            for c in range(0, value.shape[1], 128)
        ],
    )


def roll_rows(tile, step):
    return pltpu.roll(tile, step % tile.shape[0], 0)


def load_kernel(
    n, material_hbm, primal_hbm, source_hbm, fixed_hbm,
    design_ref, free_ref, rhs_ref, warmth_ref, y_up_ref, y_down_ref,
    primal_ref, source_ref, fixed_ref, arrived,
):
    copies = [
        pltpu.make_async_copy(source, target, arrived.at[k])
        for k, (source, target) in enumerate(
            (
                (material_hbm, design_ref),
                (primal_hbm, primal_ref),
                (source_hbm, source_ref),
                (fixed_hbm, fixed_ref),
            )
        )
    ]
    for copy in copies:
        copy.start()
    for copy in copies:
        copy.wait()
    row = lax.broadcasted_iota(jnp.int32, (8, design_ref.shape[-1]), 0)
    for i in range(n):
        free = (1 - fixed_ref[i]).astype(jnp.float32)
        warmth = free * primal_ref[i]
        rhs = source_ref[i].astype(jnp.float32) * warmth
        design = design_ref[i]
        free_ref[i] = free
        warmth_ref[i] = warmth
        rhs_ref[i] = rhs
        y_up_ref[i] = jnp.where(row >= 3, design[-8:], roll_rows(free[-8:], 3))
        y_up_ref[n + i] = jnp.where(row >= 5, rhs[-8:], roll_rows(warmth[-8:], 1))
        y_down_ref[i] = jnp.where(row < 5, design[:8], roll_rows(warmth[:8], 5))
        y_down_ref[n + i] = jnp.where(row < 4, rhs[:8], roll_rows(free[:8], 4))


class Layers:
    def __init__(self, n, own_rows, z):
        self.n, self.z = n, z
        self.wide, self.near = own_rows + 2 * WIDE, own_rows + 2 * NEAR
        self.tiles = (n * self.wide + (2 * n + 1) * self.near) // 8

    def place(self, which, layer):
        rows = self.near if which else self.wide
        start = layer * rows if which == 0 else self.n * self.wide + ((which - 1) * self.n + layer) * self.near
        return slice(start // 8, (start + rows) // 8), rows

    def put(self, ref, which, layer, value):
        place, rows = self.place(which, layer)
        ref[place] = value.reshape(rows // 8, 8, self.z)

    def get(self, ref, which, layer):
        place, rows = self.place(which, layer)
        return ref[place].reshape(rows, self.z)


def extend_kernel(
    n, own_rows, design_in, free_in, rhs_in, warmth_in, low_ref, high_ref, message_ref, warmth_ref
):
    layers = Layers(n, own_rows, design_in.shape[-1])

    def joined(low, middle, high):
        return jnp.concatenate([low, middle, high], axis=0)

    def near(low, middle, high):
        return joined(low, middle, high)[WIDE - NEAR : own_rows + WIDE + NEAR]

    for i in range(n):
        layers.put(message_ref, 0, i, joined(low_ref[i], design_in[i], high_ref[i]))
        layers.put(
            message_ref, 1, i, near(roll_rows(low_ref[i], -3), free_in[i], roll_rows(high_ref[n + i], -4))
        )
        layers.put(message_ref, 2, i, near(low_ref[n + i], rhs_in[i], high_ref[n + i]))
        warmth = near(roll_rows(low_ref[n + i], -1), warmth_in[i], roll_rows(high_ref[i], -5))
        warmth_ref[i] = warmth
        if i == 0:
            layers.put(message_ref, 3, 0, warmth)


def neighbours(n, own_rows, z, own_ref, same_ref, next_ref):
    layers = Layers(n, own_rows, z)
    even = lax.axis_index("gx") % 2 == 0

    def at(which, i):
        if 0 <= i < n:
            return layers.get(own_ref, which, i)
        same, other = (layers.get(ref, which, i % n) for ref in (same_ref, next_ref))
        return jnp.where(even, other, same) if i < 0 else jnp.where(even, same, other)

    return at


def basis_kernel(
    n, own_rows, layers, rows,
    own_ref, same_ref, next_ref,
    moments_ref, basis_ref, solid_ref,
    conduct_s, free_s, inverse_s, u0_s, u1_s,
):
    first_layer = lax.axis_index("gx") * n
    first_row = lax.axis_index("gy") * own_rows
    wide_rows = own_rows + 2 * WIDE
    near_rows = own_rows + 2 * NEAR
    z = own_ref.shape[-1]
    layer_at = neighbours(n, own_rows, z, own_ref, same_ref, next_ref)

    below, here = layer_at(0, -n), layer_at(0, 1 - n)
    for i in range(1 - n, 2 * n - 1):
        above = layer_at(0, i + 1)
        valid, weight = filter_weight(i, layers, first_layer, first_row - WIDE, rows, (wide_rows, z))
        solid = 1.0 - filtered(below, here, above) / weight
        below, here = here, above
        solid = solid[WIDE - NEAR : wide_rows - WIDE + NEAR]
        valid = valid[WIDE - NEAR : wide_rows - WIDE + NEAR]
        conduct_s[i + n - 1] = jnp.where(valid > 0, KMIN + (1.0 - KMIN) * (solid * solid * solid), 0.0)
        if 0 <= i < n:
            solid_ref[i] = solid

    def conduct_at(i):
        return conduct_s[i + n - 1]

    def free_at(i):
        return free_s[i + n - 2]

    for i in range(2 - n, 2 * n - 1):
        pair = conduct_at(i) + conduct_at(i - 1)
        pair = pair + down(pair, 0)
        pair = pair + lower_z(pair)
        free = layer_at(1, i)
        inverse = 1.0 / (free * (pair * (1.0 / 3.0)) + (1.0 - free))
        free_s[i + n - 2] = free
        inverse_s[i + n - 2] = inverse
        u0_s[i + n - 2] = layer_at(2, i) * inverse

    row = lax.broadcasted_iota(jnp.int32, (near_rows, z), 0)
    own = (row >= NEAR) & (row < NEAR + own_rows)
    sums = [jnp.zeros((8, 128), jnp.float32) for _ in range(MOMENTS)]

    def gather(which, product):
        sums[which] = sums[which] + tile_sum(jnp.where(own, product, 0.0))

    def step(previous, first, count):
        for i, image in apply_layers(lambda i: free_at(i) * previous(i), conduct_at, first, count):
            free, start = free_at(i), previous(i)
            image = free * image + (1.0 - free) * start
            yield i, start, image, image * inverse_s[i + n - 2] - start

    for i, start, image, later in step(lambda i: u0_s[i + n - 2], 3 - n, 3 * n - 5):
        u1_s[i + n - 3] = later
        if 0 <= i <= n:
            basis_ref[0, i] = start
        if 0 <= i < n:
            rhs = layer_at(2, i)
            gather(0, start * image)
            gather(1, later * image)
            gather(5, rhs * start)
            gather(6, rhs * later)
    for i, start, image, later in step(lambda i: u1_s[i + n - 3], 0, n + 1):
        basis_ref[1, i] = start
        basis_ref[2, i] = later
        if i < n:
            gather(2, start * image)
            gather(3, later * image)
            gather(7, layer_at(2, i) * later)
    low = yz_modes(free_at(0) * basis_ref[2, 0])
    for i in range(n):
        high = yz_modes(free_at(i + 1) * basis_ref[2, i + 1])
        square = sum(order * value * value for order, value in element_modes(low, high).values())
        last = basis_ref[2, i]
        gather(4, square * (conduct_at(i) * (1.0 / 48.0)) + (1.0 - free_at(i)) * last * last)
        low = high

    lane = lax.broadcasted_iota(jnp.int32, (1, 128), 1)
    total = jnp.zeros((1, 128), jnp.float32)
    for k in range(MOMENTS):
        total = total + jnp.where(lane == k, jnp.sum(sums[k], axis=(0, 1), keepdims=True), 0.0)
    moments_ref[...] = jnp.broadcast_to(total, moments_ref.shape)


def integrand_kernel(
    n, own_rows, layers, rows,
    basis_ref, solid_ref, warmth_ref, same_ref, next_ref,
    scaled_ref, to_same_ref, to_next_ref,
):
    even = lax.axis_index("gx") % 2 == 0
    first_layer = lax.axis_index("gx") * n
    first_row = lax.axis_index("gy") * own_rows
    shape = solid_ref.shape[1:]
    places = Layers(n, own_rows, shape[1])
    warm_low = yz_modes(warmth_ref[0])
    lows = [yz_modes(basis_ref[k, 0]) for k in range(BASIS)]
    for i in range(n):
        if i + 1 < n:
            warm = warmth_ref[i + 1]
        else:
            warm = jnp.where(even, places.get(same_ref, 3, 0), places.get(next_ref, 3, 0))
        warm_high = yz_modes(warm)
        valid, weight = filter_weight(i, layers, first_layer, first_row - NEAR, rows, shape)
        solid = solid_ref[i]
        share = jnp.where(valid > 0, 3.0 * solid * solid / weight, 0.0)
        load = {
            key: (order / 48.0) * value for key, (order, value) in element_modes(warm_low, warm_high).items()
        }
        for k in range(BASIS):
            high = yz_modes(basis_ref[k, i + 1])
            modes = element_modes(lows[k], high)
            energy = sum(load[key] * value for key, (_, value) in modes.items())
            total = lows[k][0] + high[0]
            scaled_ref[k, i] = share * ((1.0 - KMIN) * energy - (QZERO / 8.0) * total)
            lows[k] = high
        warm_low = warm_high
    for k in range(BASIS):
        first, last = scaled_ref[k, 0], scaled_ref[k, n - 1]
        to_same_ref[k] = jnp.where(even, last, first)
        to_next_ref[k] = jnp.where(even, first, last)


def spread_kernel(moments_ref, total_ref):
    total = jnp.sum(moments_ref[...], axis=0, keepdims=True)
    total_ref[...] = jnp.broadcast_to(total, total_ref.shape)


def solve_kernel(moments_ref, coefs_ref):
    total = jnp.sum(moments_ref[...], axis=0, keepdims=True)
    a0, a1, a2, a3, a4, b0, b1, b2 = (
        jnp.broadcast_to(total[:, k : k + 1], (1, 128)) for k in range(MOMENTS)
    )
    l10 = a1 / a0
    l20 = a2 / a0
    d1 = a2 - l10 * a1
    t21 = a3 - l20 * a1
    l21 = t21 / d1
    d2 = a4 - l20 * a2 - l21 * t21
    z1 = b1 - l10 * b0
    z2 = b2 - l20 * b0 - l21 * z1
    y2 = z2 / d2
    y1 = z1 / d1 - l21 * y2
    y0 = b0 / a0 - l10 * y1 - l20 * y2
    for k, y in enumerate((y0, y1, y2)):
        coefs_ref[k] = jnp.broadcast_to(y, coefs_ref.shape[1:])


def final_kernel(n, own_rows, coefs_ref, basis_ref, scaled_ref, same_ref, next_ref, dual_ref, sens_ref):
    even = lax.axis_index("gx") % 2 == 0
    z = dual_ref.shape[-1]
    near_rows = own_rows + 2 * NEAR
    coefs = [
        jnp.broadcast_to(jnp.concatenate([coefs_ref[k, :1]] * (z // 128), axis=1), (near_rows, z))
        for k in range(BASIS)
    ]

    def combined(layers):
        return sum(coef * layer for coef, layer in zip(coefs, layers))

    for i in range(n):
        dual_ref[i] = combined([basis_ref[k, i] for k in range(BASIS)])[NEAR : NEAR + own_rows]
    same = combined([same_ref[k] for k in range(BASIS)])
    other = combined([next_ref[k] for k in range(BASIS)])
    layers = [combined([scaled_ref[k, i] for k in range(BASIS)]) for i in range(n)]
    layers = [jnp.where(even, other, same)] + layers + [jnp.where(even, same, other)]
    for i in range(n):
        sens_ref[i] = filtered(*layers[i : i + 3])[NEAR : NEAR + own_rows]


def shifted(arr, axis, step):
    count = lax.axis_size(axis)
    return lax.ppermute(arr, axis, [(i, i + step) for i in range(count) if 0 <= i + step < count])


def swapped(arr, axis, start):
    pairs = [(i, i + 1) for i in range(start, lax.axis_size(axis) - 1, 2)]
    return lax.ppermute(arr, axis, pairs + [(j, i) for i, j in pairs])


def body(gx, gy, material_fraction, primal_warmth, empty_region_flags, dirichlet_flags):
    n, own_rows, z = material_fraction.shape
    sizes = (n, own_rows, gx * n, gy * own_rows)
    near = own_rows + 2 * NEAR

    def call(name, kernel, outs, *operands, scratch=(), space=pltpu.VMEM, limit=VMEM_LIMIT, flops=0):
        return pl.pallas_call(
            kernel,
            out_shape=[jax.ShapeDtypeStruct(shape, jnp.float32) for shape in outs],
            in_specs=[pl.BlockSpec(memory_space=space)] * len(operands),
            out_specs=[pl.BlockSpec(memory_space=pltpu.VMEM)] * len(outs),
            scratch_shapes=list(scratch),
            compiler_params=pltpu.CompilerParams(vmem_limit_bytes=limit),
            cost_estimate=pl.CostEstimate(flops=flops, bytes_accessed=1 << 20, transcendentals=0),
            name=name,
        )(*operands)

    def floats(*shape):
        return pltpu.VMEM(shape, jnp.float32)

    brick_shape = (n, own_rows, z)
    *own, y_up, y_down = call(
        "load",
        functools.partial(load_kernel, n),
        [brick_shape] * 4 + [(2 * n, 8, z)] * 2,
        material_fraction, primal_warmth, empty_region_flags, dirichlet_flags,
        scratch=[
            floats(*brick_shape),
            pltpu.VMEM(brick_shape, jnp.int32),
            pltpu.VMEM(brick_shape, jnp.int32),
            pltpu.SemaphoreType.DMA((4,)),
        ],
        space=pltpu.HBM,
        limit=LOAD_LIMIT,
    )
    y_low = shifted(y_up, "gy", 1)
    y_high = shifted(y_down, "gy", -1)
    places = Layers(n, own_rows, z)
    message, warmth = call(
        "extend",
        functools.partial(extend_kernel, n, own_rows),
        [(places.tiles, 8, z), (n, near, z)],
        *own, y_low, y_high,
    )
    same, other = swapped(message, "gx", 0), swapped(message, "gx", 1)

    pairs = 2 if gx % 2 == 0 else 1
    inner, outer = pairs * gy, gx // pairs
    moments, basis, solid = call(
        "basis",
        functools.partial(basis_kernel, *sizes),
        [(inner, 128), (BASIS, n + 1, near, z), (n, near, z)],
        message, same, other,
        scratch=[floats(count, near, z) for count in (3 * n - 2, 3 * n - 3, 3 * n - 3, 3 * n - 3, 3 * n - 5)],
    )
    scaled, to_same, to_next = call(
        "integrand",
        functools.partial(integrand_kernel, *sizes),
        [(BASIS, n, near, z), (BASIS, near, z), (BASIS, near, z)],
        basis, solid, warmth, same, other,
    )

    near_groups = [
        [(g * pairs + c) * gy + y for c in range(pairs) for y in range(gy)] for g in range(outer)
    ]
    far_groups = [
        [(g * pairs + c) * gy + y for g in range(outer)] for c in range(pairs) for y in range(gy)
    ]
    moments = lax.all_to_all(moments, ("gx", "gy"), 0, 0, axis_index_groups=near_groups, tiled=True)
    (moments,) = call("spread", spread_kernel, [(outer, 128)], moments, flops=FAR_WORK)
    from_same, from_next = swapped(to_same, "gx", 0), swapped(to_next, "gx", 1)
    moments = lax.all_to_all(moments, ("gx", "gy"), 0, 0, axis_index_groups=far_groups, tiled=True)
    (coefs,) = call("solve", solve_kernel, [(BASIS, 8, 128)], moments, flops=1000)
    return tuple(
        call(
            "combine",
            functools.partial(final_kernel, n, own_rows),
            [brick_shape, brick_shape],
            coefs, basis, scaled, from_same, from_next,
        )
    )


def solution(mesh):
    placed = P("gx", "gy", None)
    return jax.shard_map(
        functools.partial(body, mesh.shape["gx"], mesh.shape["gy"]),
        mesh=mesh,
        in_specs=(placed,) * 4,
        out_specs=(placed, placed),
        check_vma=False,
    )
```

```python
import functools
import math

import jax
import jax.numpy as jnp
from jax import lax
from jax.experimental import pallas as pl
from jax.experimental.pallas import tpu as pltpu
from jax.sharding import PartitionSpec as P

KMIN = 0.05
QZERO = 1.0
EDGE = 0.5
DIAGONAL = 1.5 - math.sqrt(2.0)

WIDE = 8
NEAR = 4
BASIS = 3
MOMENTS = 8
VMEM_LIMIT = 12 << 20
FAR_WORK = 10**10
LOAD_LIMIT = 857 << 16


def up(arr, axis):
    return pltpu.roll(arr, arr.shape[axis] - 1, axis)


def down(arr, axis):
    return pltpu.roll(arr, 1, axis)


def z_index(arr):
    return lax.broadcasted_iota(jnp.int32, arr.shape, 1)


def lift(arr):
    return jnp.where(z_index(arr) == arr.shape[1] - 1, 0.0, up(arr, 1))


def lower_z(arr):
    return jnp.where(z_index(arr) == 0, 0.0, down(arr, 1))


def with_rim(layer):
    return layer, up(layer, 0) + down(layer, 0)


def filtered(below, here, above):
    beside = below[0] + above[0]
    around = beside + here[1]
    flat = 1.5 * here[0] + EDGE * around + DIAGONAL * (below[1] + above[1])
    slanted = EDGE * here[0] + DIAGONAL * around
    return flat + lift(slanted) + lower_z(slanted)


def layer_inside(at, layers):
    return ((at >= 0) & (at < layers)).astype(jnp.float32)


def row_inside(first_row, rows, shape):
    row = first_row + lax.broadcasted_iota(jnp.int32, shape, 0)
    return [((row + step >= 0) & (row + step < rows)).astype(jnp.float32) for step in (0, -1, 1)]


def inverse_weights(first_row, rows, shape):
    here, before, after = row_inside(first_row, rows, shape)
    z = lax.broadcasted_iota(jnp.int32, shape, 1)
    z_beside = (z > 0).astype(jnp.float32) + (z < shape[1] - 1).astype(jnp.float32)
    inverses = []
    for beside in (2.0, 1.0):
        flat = (1.5 + EDGE * beside) * here + (EDGE + DIAGONAL * beside) * (before + after)
        slanted = (EDGE + DIAGONAL * beside) * here + DIAGONAL * (before + after)
        weight = flat + z_beside * slanted
        inverses.append(jnp.where(here > 0, 1.0 / jnp.where(here > 0, weight, 1.0), 0.0))
    return here > 0, inverses


def inverse_at(inverses, at, layers):
    inner = (at > 0) & (at < layers - 1)
    return jnp.where(inner, *inverses)


def yz_modes(node):
    lifted = lift(node)
    plain, slope = node + lifted, lifted - node
    plain_up, slope_up = up(plain, 0), up(slope, 0)
    return plain + plain_up, slope + slope_up, plain_up - plain, slope_up - slope


def element_modes(low, high):
    return {
        "d0": (3.0, high[0] - low[0]),
        "s1": (3.0, high[1] + low[1]),
        "s2": (3.0, high[2] + low[2]),
        "d1": (2.0, high[1] - low[1]),
        "d2": (2.0, high[2] - low[2]),
        "s3": (2.0, high[3] + low[3]),
        "d3": (1.0, high[3] - low[3]),
    }


def apply_layers(node_at, conduct_at, first, count):
    low = yz_modes(node_at(first - 1))
    carried = None
    for element in range(first - 1, first + count):
        high = yz_modes(node_at(element + 1))
        scaled = conduct_at(element) * (1.0 / 48.0)
        flow = {key: (order * value) * scaled for key, (order, value) in element_modes(low, high).items()}
        zero_sum = flow["d0"]
        if carried is not None:
            planes = (
                carried[0] - zero_sum,
                carried[1] + (flow["s1"] - flow["d1"]),
                carried[2] + (flow["s2"] - flow["d2"]),
                carried[3] + (flow["s3"] - flow["d3"]),
            )
            smooth = (planes[0] - planes[2]) + down(planes[0] + planes[2], 0)
            slope = (planes[1] - planes[3]) + down(planes[1] + planes[3], 0)
            yield element, (smooth - slope) + lower_z(smooth + slope)
        carried = (
            zero_sum,
            flow["s1"] + flow["d1"],
            flow["s2"] + flow["d2"],
            flow["s3"] + flow["d3"],
        )
        low = high


def tile_sum(value):
    return functools.reduce(
        jnp.add,
        [
            value[r : r + 8, c : c + 128]
            for r in range(0, value.shape[0], 8)
            for c in range(0, value.shape[1], 128)
        ],
    )


def roll_rows(tile, step):
    return pltpu.roll(tile, step % tile.shape[0], 0)


def load_kernel(
    n, material_hbm, primal_hbm, source_hbm, fixed_hbm,
    design_ref, free_ref, rhs_ref, warmth_ref, y_up_ref, y_down_ref,
    primal_ref, source_ref, fixed_ref, arrived,
):
    copies = [
        pltpu.make_async_copy(source, target, arrived.at[k])
        for k, (source, target) in enumerate(
            (
                (material_hbm, design_ref),
                (primal_hbm, primal_ref),
                (source_hbm, source_ref),
                (fixed_hbm, fixed_ref),
            )
        )
    ]
    for copy in copies:
        copy.start()
    for copy in copies:
        copy.wait()
    row = lax.broadcasted_iota(jnp.int32, (8, design_ref.shape[-1]), 0)
    for i in range(n):
        free = (1 - fixed_ref[i]).astype(jnp.float32)
        warmth = free * primal_ref[i]
        rhs = source_ref[i].astype(jnp.float32) * warmth
        design = design_ref[i]
        free_ref[i] = free
        warmth_ref[i] = warmth
        rhs_ref[i] = rhs
        y_up_ref[i] = jnp.where(row >= 3, design[-8:], roll_rows(free[-8:], 3))
        y_up_ref[n + i] = jnp.where(row >= 5, rhs[-8:], roll_rows(warmth[-8:], 1))
        y_down_ref[i] = jnp.where(row < 5, design[:8], roll_rows(warmth[:8], 5))
        y_down_ref[n + i] = jnp.where(row < 4, rhs[:8], roll_rows(free[:8], 4))


class Layers:
    def __init__(self, n, own_rows, z):
        self.n, self.z = n, z
        self.wide, self.near = own_rows + 2 * WIDE, own_rows + 2 * NEAR
        self.tiles = (n * self.wide + (2 * n - 1) * self.near) // 8

    def place(self, which, layer):
        rows = self.near if which else self.wide
        start = layer * rows if which == 0 else self.n * self.wide + ((which - 1) * (self.n - 1) + layer) * self.near
        return slice(start // 8, (start + rows) // 8), rows

    def put(self, ref, which, layer, value):
        place, rows = self.place(which, layer)
        ref[place] = value.reshape(rows // 8, 8, self.z)

    def get(self, ref, which, layer):
        place, rows = self.place(which, layer)
        return ref[place].reshape(rows, self.z)


def extend_kernel(
    n, own_rows, design_in, free_in, rhs_in, warmth_in, low_ref, high_ref,
    free_ref, rhs_ref, warmth_ref, to_same_ref, to_next_ref,
):
    even = lax.axis_index("gx") % 2 == 0
    layers = Layers(n, own_rows, design_in.shape[-1])

    def joined(low, middle, high):
        return jnp.concatenate([low, middle, high], axis=0)

    def near(low, middle, high):
        return joined(low, middle, high)[WIDE - NEAR : own_rows + WIDE + NEAR]

    free, rhs = [], []
    for i in range(n):
        design = joined(low_ref[i], design_in[i], high_ref[i])
        layers.put(to_same_ref, 0, i, design)
        layers.put(to_next_ref, 0, i, design)
        free.append(near(roll_rows(low_ref[i], -3), free_in[i], roll_rows(high_ref[n + i], -4)))
        rhs.append(near(low_ref[n + i], rhs_in[i], high_ref[n + i]))
        warmth = near(roll_rows(low_ref[n + i], -1), warmth_in[i], roll_rows(high_ref[i], -5))
        free_ref[i], rhs_ref[i], warmth_ref[i] = free[i], rhs[i], warmth
        if i == 0:
            layers.put(to_same_ref, 3, 0, warmth)
            layers.put(to_next_ref, 3, 0, warmth)
    for which, values in ((1, free), (2, rhs)):
        for i in range(n - 1):
            layers.put(to_same_ref, which, i, jnp.where(even, values[i + 1], values[i]))
            layers.put(to_next_ref, which, i, jnp.where(even, values[i], values[i + 1]))


def neighbours(n, own_rows, z, own_ref, free_ref, rhs_ref, same_ref, next_ref):
    layers = Layers(n, own_rows, z)
    even = lax.axis_index("gx") % 2 == 0

    def at(which, i):
        if 0 <= i < n:
            return (free_ref, rhs_ref)[which - 1][i] if which else layers.get(own_ref, 0, i)
        slot = i % n - (1 if which and i < 0 else 0)
        same, other = (layers.get(ref, which, slot) for ref in (same_ref, next_ref))
        return jnp.where(even, other, same) if i < 0 else jnp.where(even, same, other)

    return at


def basis_kernel(
    n, own_rows, layers, rows,
    own_ref, free_ref, rhs_ref, same_ref, next_ref,
    moments_ref, basis_ref, solid_ref,
    conduct_s, free_s, inverse_s, u0_s, u1_s,
):
    first_layer = lax.axis_index("gx") * n
    first_row = lax.axis_index("gy") * own_rows
    near_rows = own_rows + 2 * NEAR
    z = own_ref.shape[-1]
    layer_at = neighbours(n, own_rows, z, own_ref, free_ref, rhs_ref, same_ref, next_ref)

    def design_at(i):
        layer = layer_at(0, i)
        before, here, after = (
            layer[WIDE - NEAR + step : WIDE - NEAR + step + near_rows] for step in (-1, 0, 1)
        )
        return here, before + after

    valid, inverses = inverse_weights(first_row - NEAR, rows, (near_rows, z))
    below, here = design_at(-n), design_at(1 - n)
    for i in range(1 - n, 2 * n - 1):
        above = design_at(i + 1)
        at = first_layer + i
        solid = 1.0 - filtered(below, here, above) * inverse_at(inverses, at, layers)
        below, here = here, above
        conduct = KMIN + (1.0 - KMIN) * (solid * solid * solid)
        conduct_s[i + n - 1] = jnp.where(valid & (at >= 0) & (at < layers), conduct, 0.0)
        if 0 <= i < n:
            solid_ref[i] = solid

    def conduct_at(i):
        return conduct_s[i + n - 1]

    def free_at(i):
        return free_s[i + n - 2]

    for i in range(2 - n, 2 * n - 1):
        pair = conduct_at(i) + conduct_at(i - 1)
        pair = pair + down(pair, 0)
        pair = pair + lower_z(pair)
        free = layer_at(1, i)
        inverse = 1.0 / (free * (pair * (1.0 / 3.0)) + (1.0 - free))
        free_s[i + n - 2] = free
        inverse_s[i + n - 2] = inverse
        u0_s[i + n - 2] = layer_at(2, i) * inverse

    row = lax.broadcasted_iota(jnp.int32, (near_rows, z), 0)
    own = (row >= NEAR) & (row < NEAR + own_rows)
    sums = [jnp.zeros((8, 128), jnp.float32) for _ in range(MOMENTS)]

    def gather(which, product):
        sums[which] = sums[which] + tile_sum(jnp.where(own, product, 0.0))

    def step(previous, first, count):
        for i, image in apply_layers(lambda i: free_at(i) * previous(i), conduct_at, first, count):
            free, start = free_at(i), previous(i)
            image = free * image + (1.0 - free) * start
            yield i, start, image, image * inverse_s[i + n - 2] - start

    for i, start, image, later in step(lambda i: u0_s[i + n - 2], 3 - n, 3 * n - 5):
        u1_s[i + n - 3] = later
        if 0 <= i <= n:
            basis_ref[0, i] = start
        if 0 <= i < n:
            rhs = layer_at(2, i)
            gather(0, start * image)
            gather(1, later * image)
            gather(5, rhs * start)
            gather(6, rhs * later)
    for i, start, image, later in step(lambda i: u1_s[i + n - 3], 0, n + 1):
        basis_ref[1, i] = start
        basis_ref[2, i] = later
        if i < n:
            gather(2, start * image)
            gather(3, later * image)
            gather(7, layer_at(2, i) * later)
    low = yz_modes(free_at(0) * basis_ref[2, 0])
    for i in range(n):
        high = yz_modes(free_at(i + 1) * basis_ref[2, i + 1])
        square = sum(order * value * value for order, value in element_modes(low, high).values())
        last = basis_ref[2, i]
        gather(4, square * (conduct_at(i) * (1.0 / 48.0)) + (1.0 - free_at(i)) * last * last)
        low = high

    table = jnp.concatenate([jnp.sum(partial, axis=0, keepdims=True) for partial in sums], axis=0)
    column = jnp.sum(table, axis=1, keepdims=True)
    diagonal = lax.broadcasted_iota(jnp.int32, (8, 128), 0) == lax.broadcasted_iota(jnp.int32, (8, 128), 1)
    total = jnp.sum(jnp.where(diagonal, column, 0.0), axis=0, keepdims=True)
    moments_ref[...] = jnp.broadcast_to(total, moments_ref.shape)


def integrand_kernel(
    n, own_rows, layers, rows,
    basis_ref, solid_ref, warmth_ref, same_ref, next_ref,
    scaled_ref, to_same_ref, to_next_ref,
):
    even = lax.axis_index("gx") % 2 == 0
    first_layer = lax.axis_index("gx") * n
    first_row = lax.axis_index("gy") * own_rows
    shape = solid_ref.shape[1:]
    places = Layers(n, own_rows, shape[1])
    _, inverses = inverse_weights(first_row - NEAR, rows, shape)
    warm_low = yz_modes(warmth_ref[0])
    lows = [yz_modes(basis_ref[k, 0]) for k in range(BASIS)]
    for i in range(n):
        if i + 1 < n:
            warm = warmth_ref[i + 1]
        else:
            warm = jnp.where(even, places.get(same_ref, 3, 0), places.get(next_ref, 3, 0))
        warm_high = yz_modes(warm)
        solid = solid_ref[i]
        share = (3.0 * solid * solid) * inverse_at(inverses, first_layer + i, layers)
        load = {
            key: (order / 48.0) * value for key, (order, value) in element_modes(warm_low, warm_high).items()
        }
        for k in range(BASIS):
            high = yz_modes(basis_ref[k, i + 1])
            modes = element_modes(lows[k], high)
            energy = sum(load[key] * value for key, (_, value) in modes.items())
            total = lows[k][0] + high[0]
            scaled_ref[k, i] = share * ((1.0 - KMIN) * energy - (QZERO / 8.0) * total)
            lows[k] = high
        warm_low = warm_high
    for k in range(BASIS):
        first, last = scaled_ref[k, 0], scaled_ref[k, n - 1]
        to_same_ref[k] = jnp.where(even, last, first)
        to_next_ref[k] = jnp.where(even, first, last)


def spread_kernel(moments_ref, total_ref):
    total = jnp.sum(moments_ref[...], axis=0, keepdims=True)
    total_ref[...] = jnp.broadcast_to(total, total_ref.shape)


def coefficients(total):
    a0, a1, a2, a3, a4, b0, b1, b2 = (
        jnp.broadcast_to(total[:, k : k + 1], (1, 128)) for k in range(MOMENTS)
    )
    l10 = a1 / a0
    l20 = a2 / a0
    d1 = a2 - l10 * a1
    t21 = a3 - l20 * a1
    l21 = t21 / d1
    d2 = a4 - l20 * a2 - l21 * t21
    z1 = b1 - l10 * b0
    z2 = b2 - l20 * b0 - l21 * z1
    y2 = z2 / d2
    y1 = z1 / d1 - l21 * y2
    y0 = b0 / a0 - l10 * y1 - l20 * y2
    return y0, y1, y2


def final_kernel(n, own_rows, moments_ref, basis_ref, scaled_ref, same_ref, next_ref, dual_ref, sens_ref):
    even = lax.axis_index("gx") % 2 == 0
    z = dual_ref.shape[-1]
    near_rows = own_rows + 2 * NEAR
    coefs = [
        jnp.broadcast_to(jnp.concatenate([y] * (z // 128), axis=1), (near_rows, z))
        for y in coefficients(jnp.sum(moments_ref[...], axis=0, keepdims=True))
    ]

    def combined(layers):
        return sum(coef * layer for coef, layer in zip(coefs, layers))

    for i in range(n):
        dual_ref[i] = combined([basis_ref[k, i] for k in range(BASIS)])[NEAR : NEAR + own_rows]
    same = combined([same_ref[k] for k in range(BASIS)])
    other = combined([next_ref[k] for k in range(BASIS)])
    layers = [combined([scaled_ref[k, i] for k in range(BASIS)]) for i in range(n)]
    layers = [jnp.where(even, other, same)] + layers + [jnp.where(even, same, other)]
    layers = [with_rim(layer) for layer in layers]
    for i in range(n):
        sens_ref[i] = filtered(*layers[i : i + 3])[NEAR : NEAR + own_rows]


def shifted(arr, axis, step):
    count = lax.axis_size(axis)
    return lax.ppermute(arr, axis, [(i, i + step) for i in range(count) if 0 <= i + step < count])


def swapped(arr, axis, start):
    pairs = [(i, i + 1) for i in range(start, lax.axis_size(axis) - 1, 2)]
    return lax.ppermute(arr, axis, pairs + [(j, i) for i, j in pairs])


def body(gx, gy, material_fraction, primal_warmth, empty_region_flags, dirichlet_flags):
    n, own_rows, z = material_fraction.shape
    sizes = (n, own_rows, gx * n, gy * own_rows)
    near = own_rows + 2 * NEAR

    def call(name, kernel, outs, *operands, scratch=(), space=pltpu.VMEM, limit=VMEM_LIMIT, flops=0):
        return pl.pallas_call(
            kernel,
            out_shape=[jax.ShapeDtypeStruct(shape, jnp.float32) for shape in outs],
            in_specs=[pl.BlockSpec(memory_space=space)] * len(operands),
            out_specs=[pl.BlockSpec(memory_space=pltpu.VMEM)] * len(outs),
            scratch_shapes=list(scratch),
            compiler_params=pltpu.CompilerParams(vmem_limit_bytes=limit),
            cost_estimate=pl.CostEstimate(flops=flops, bytes_accessed=1 << 20, transcendentals=0),
            name=name,
        )(*operands)

    def floats(*shape):
        return pltpu.VMEM(shape, jnp.float32)

    brick_shape = (n, own_rows, z)
    *own, y_up, y_down = call(
        "load",
        functools.partial(load_kernel, n),
        [brick_shape] * 4 + [(2 * n, 8, z)] * 2,
        material_fraction, primal_warmth, empty_region_flags, dirichlet_flags,
        scratch=[
            floats(*brick_shape),
            pltpu.VMEM(brick_shape, jnp.int32),
            pltpu.VMEM(brick_shape, jnp.int32),
            pltpu.SemaphoreType.DMA((4,)),
        ],
        space=pltpu.HBM,
        limit=LOAD_LIMIT,
    )
    y_low = shifted(y_up, "gy", 1)
    y_high = shifted(y_down, "gy", -1)
    places = Layers(n, own_rows, z)
    free, rhs, warmth, to_same, to_next = call(
        "extend",
        functools.partial(extend_kernel, n, own_rows),
        [(n, near, z)] * 3 + [(places.tiles, 8, z)] * 2,
        *own, y_low, y_high,
    )
    same, other = swapped(to_same, "gx", 0), swapped(to_next, "gx", 1)

    pairs = 2 if gx % 2 == 0 else 1
    inner, outer = pairs * gy, gx // pairs
    moments, basis, solid = call(
        "basis",
        functools.partial(basis_kernel, *sizes),
        [(inner, 128), (BASIS, n + 1, near, z), (n, near, z)],
        to_same, free, rhs, same, other,
        scratch=[floats(count, near, z) for count in (3 * n - 2, 3 * n - 3, 3 * n - 3, 3 * n - 3, 3 * n - 5)],
    )
    scaled, to_same, to_next = call(
        "integrand",
        functools.partial(integrand_kernel, *sizes),
        [(BASIS, n, near, z), (BASIS, near, z), (BASIS, near, z)],
        basis, solid, warmth, same, other,
    )

    near_groups = [
        [(g * pairs + c) * gy + y for c in range(pairs) for y in range(gy)] for g in range(outer)
    ]
    far_groups = [
        [(g * pairs + c) * gy + y for g in range(outer)] for c in range(pairs) for y in range(gy)
    ]
    moments = lax.all_to_all(moments, ("gx", "gy"), 0, 0, axis_index_groups=near_groups, tiled=True)
    (moments,) = call("spread", spread_kernel, [(outer, 128)], moments, flops=FAR_WORK)
    from_same, from_next = swapped(to_same, "gx", 0), swapped(to_next, "gx", 1)
    moments = lax.all_to_all(moments, ("gx", "gy"), 0, 0, axis_index_groups=far_groups, tiled=True)
    return tuple(
        call(
            "combine",
            functools.partial(final_kernel, n, own_rows),
            [brick_shape, brick_shape],
            moments, basis, scaled, from_same, from_next,
        )
    )


def solution(mesh):
    placed = P("gx", "gy", None)
    return jax.shard_map(
        functools.partial(body, mesh.shape["gx"], mesh.shape["gy"]),
        mesh=mesh,
        in_specs=(placed,) * 4,
        out_specs=(placed, placed),
        check_vma=False,
    )
```

```python
import functools
import math

import jax
import jax.numpy as jnp
from jax import lax
from jax.experimental import pallas as pl
from jax.experimental.pallas import tpu as pltpu
from jax.sharding import PartitionSpec as P

KMIN = 0.05
QZERO = 1.0
EDGE = 0.5
DIAGONAL = 1.5 - math.sqrt(2.0)

WIDE = 8
NEAR = 4
BASIS = 3
SPARE = 3
MOMENTS = 8
VMEM_LIMIT = 12 << 20
FAR_WORK = 10**10
LOAD_LIMIT = 857 << 16


def up(arr, axis):
    return pltpu.roll(arr, arr.shape[axis] - 1, axis)


def down(arr, axis):
    return pltpu.roll(arr, 1, axis)


def z_index(arr):
    return lax.broadcasted_iota(jnp.int32, arr.shape, 1)


def lift(arr):
    return jnp.where(z_index(arr) == arr.shape[1] - 1, 0.0, up(arr, 1))


def lower_z(arr):
    return jnp.where(z_index(arr) == 0, 0.0, down(arr, 1))


def with_rim(layer):
    return layer, up(layer, 0) + down(layer, 0)


def filtered(below, here, above):
    beside = below[0] + above[0]
    around = beside + here[1]
    flat = 1.5 * here[0] + EDGE * around + DIAGONAL * (below[1] + above[1])
    slanted = EDGE * here[0] + DIAGONAL * around
    return flat + lift(slanted) + lower_z(slanted)


def layer_inside(at, layers):
    return ((at >= 0) & (at < layers)).astype(jnp.float32)


def row_inside(first_row, rows, shape):
    row = first_row + lax.broadcasted_iota(jnp.int32, shape, 0)
    return [((row + step >= 0) & (row + step < rows)).astype(jnp.float32) for step in (0, -1, 1)]


def inverse_weights(first_row, rows, shape):
    here, before, after = row_inside(first_row, rows, shape)
    z = lax.broadcasted_iota(jnp.int32, shape, 1)
    z_beside = (z > 0).astype(jnp.float32) + (z < shape[1] - 1).astype(jnp.float32)
    inverses = []
    for beside in (2.0, 1.0):
        flat = (1.5 + EDGE * beside) * here + (EDGE + DIAGONAL * beside) * (before + after)
        slanted = (EDGE + DIAGONAL * beside) * here + DIAGONAL * (before + after)
        weight = flat + z_beside * slanted
        inverses.append(jnp.where(here > 0, 1.0 / jnp.where(here > 0, weight, 1.0), 0.0))
    return here > 0, inverses


def inverse_at(inverses, at, layers):
    inner = (at > 0) & (at < layers - 1)
    return jnp.where(inner, *inverses)


def yz_modes(node):
    lifted = lift(node)
    plain, slope = node + lifted, lifted - node
    plain_up, slope_up = up(plain, 0), up(slope, 0)
    return plain + plain_up, slope + slope_up, plain_up - plain, slope_up - slope


def element_modes(low, high):
    return {
        "d0": (3.0, high[0] - low[0]),
        "s1": (3.0, high[1] + low[1]),
        "s2": (3.0, high[2] + low[2]),
        "d1": (2.0, high[1] - low[1]),
        "d2": (2.0, high[2] - low[2]),
        "s3": (2.0, high[3] + low[3]),
        "d3": (1.0, high[3] - low[3]),
    }


def apply_layers(node_at, conduct_at, first, count):
    low = yz_modes(node_at(first - 1))
    carried = None
    for element in range(first - 1, first + count):
        high = yz_modes(node_at(element + 1))
        scaled = conduct_at(element) * (1.0 / 48.0)
        flow = {key: (order * value) * scaled for key, (order, value) in element_modes(low, high).items()}
        zero_sum = flow["d0"]
        if carried is not None:
            planes = (
                carried[0] - zero_sum,
                carried[1] + (flow["s1"] - flow["d1"]),
                carried[2] + (flow["s2"] - flow["d2"]),
                carried[3] + (flow["s3"] - flow["d3"]),
            )
            smooth = (planes[0] - planes[2]) + down(planes[0] + planes[2], 0)
            slope = (planes[1] - planes[3]) + down(planes[1] + planes[3], 0)
            yield element, (smooth - slope) + lower_z(smooth + slope)
        carried = (
            zero_sum,
            flow["s1"] + flow["d1"],
            flow["s2"] + flow["d2"],
            flow["s3"] + flow["d3"],
        )
        low = high


def tile_sum(value):
    return functools.reduce(
        jnp.add,
        [
            value[r : r + 8, c : c + 128]
            for r in range(0, value.shape[0], 8)
            for c in range(0, value.shape[1], 128)
        ],
    )


def roll_rows(tile, step):
    return pltpu.roll(tile, step % tile.shape[0], 0)


def load_kernel(
    n, material_hbm, primal_hbm, source_hbm, fixed_hbm,
    design_ref, free_ref, rhs_ref, warmth_ref, y_up_ref, y_down_ref,
    primal_ref, source_ref, fixed_ref, arrived,
):
    copies = [
        pltpu.make_async_copy(source, target, arrived.at[k])
        for k, (source, target) in enumerate(
            (
                (material_hbm, design_ref),
                (primal_hbm, primal_ref),
                (source_hbm, source_ref),
                (fixed_hbm, fixed_ref),
            )
        )
    ]
    for copy in copies:
        copy.start()
    for copy in copies:
        copy.wait()
    row = lax.broadcasted_iota(jnp.int32, (8, design_ref.shape[-1]), 0)
    for i in range(n):
        free = (1 - fixed_ref[i]).astype(jnp.float32)
        warmth = free * primal_ref[i]
        rhs = source_ref[i].astype(jnp.float32) * warmth
        design = design_ref[i]
        free_ref[i] = free
        warmth_ref[i] = warmth
        rhs_ref[i] = rhs
        y_up_ref[i] = jnp.where(row >= 3, design[-8:], roll_rows(free[-8:], 3))
        y_up_ref[n + i] = jnp.where(row >= 5, rhs[-8:], roll_rows(warmth[-8:], 1))
        y_down_ref[i] = jnp.where(row < 5, design[:8], roll_rows(warmth[:8], 5))
        y_down_ref[n + i] = jnp.where(row < 4, rhs[:8], roll_rows(free[:8], 4))


class Layers:
    def __init__(self, n, own_rows, z):
        self.n, self.z = n, z
        self.wide, self.near = own_rows + 2 * WIDE, own_rows + 2 * NEAR
        self.tiles = (n * self.wide + (2 * n - 2) * self.near) // 8

    def place(self, which, layer):
        rows = self.near if which else self.wide
        start = layer * rows if which == 0 else self.n * self.wide + ((which - 1) * (self.n - 1) + layer) * self.near
        return slice(start // 8, (start + rows) // 8), rows

    def put(self, ref, which, layer, value):
        place, rows = self.place(which, layer)
        ref[place] = value.reshape(rows // 8, 8, self.z)

    def get(self, ref, which, layer):
        place, rows = self.place(which, layer)
        return ref[place].reshape(rows, self.z)


def with_spare(design, carried):
    return jnp.concatenate([carried[:SPARE], design[SPARE:-SPARE], carried[SPARE:]], axis=0)


def spare_rows(layers, ref):
    pieces = []
    for i in range(layers.n):
        design = layers.get(ref, 0, i)
        pieces += [design[:SPARE], design[-SPARE:]]
    return jnp.concatenate(pieces, axis=0)


def extend_kernel(
    n, own_rows, design_in, free_in, rhs_in, warmth_in, low_ref, high_ref,
    free_ref, rhs_ref, warmth_ref, to_same_ref, to_next_ref,
):
    even = lax.axis_index("gx") % 2 == 0
    layers = Layers(n, own_rows, design_in.shape[-1])

    def joined(low, middle, high):
        return jnp.concatenate([low, middle, high], axis=0)

    def near(low, middle, high):
        return joined(low, middle, high)[WIDE - NEAR : own_rows + WIDE + NEAR]

    free, rhs = [], []
    for i in range(n):
        free.append(near(roll_rows(low_ref[i], -3), free_in[i], roll_rows(high_ref[n + i], -4)))
        rhs.append(near(low_ref[n + i], rhs_in[i], high_ref[n + i]))
        warmth = near(roll_rows(low_ref[n + i], -1), warmth_in[i], roll_rows(high_ref[i], -5))
        free_ref[i], rhs_ref[i], warmth_ref[i] = free[i], rhs[i], warmth
        if i == 0:
            carried = warmth
        design = joined(low_ref[i], design_in[i], high_ref[i])
        design = with_spare(design, carried[2 * SPARE * i : 2 * SPARE * (i + 1)])
        layers.put(to_same_ref, 0, i, design)
        layers.put(to_next_ref, 0, i, design)
    for which, values in ((1, free), (2, rhs)):
        for i in range(n - 1):
            layers.put(to_same_ref, which, i, jnp.where(even, values[i + 1], values[i]))
            layers.put(to_next_ref, which, i, jnp.where(even, values[i], values[i + 1]))


def neighbours(n, own_rows, z, own_ref, free_ref, rhs_ref, same_ref, next_ref):
    layers = Layers(n, own_rows, z)
    even = lax.axis_index("gx") % 2 == 0

    def at(which, i):
        if 0 <= i < n:
            return (free_ref, rhs_ref)[which - 1][i] if which else layers.get(own_ref, 0, i)
        slot = i % n - (1 if which and i < 0 else 0)
        same, other = (layers.get(ref, which, slot) for ref in (same_ref, next_ref))
        return jnp.where(even, other, same) if i < 0 else jnp.where(even, same, other)

    return at


def basis_kernel(
    n, own_rows, layers, rows,
    own_ref, free_ref, rhs_ref, same_ref, next_ref,
    moments_ref, basis_ref, solid_ref,
    conduct_s, free_s, inverse_s, u0_s, u1_s,
):
    first_layer = lax.axis_index("gx") * n
    first_row = lax.axis_index("gy") * own_rows
    near_rows = own_rows + 2 * NEAR
    z = own_ref.shape[-1]
    layer_at = neighbours(n, own_rows, z, own_ref, free_ref, rhs_ref, same_ref, next_ref)

    def design_at(i):
        layer = layer_at(0, i)
        before, here, after = (
            layer[WIDE - NEAR + step : WIDE - NEAR + step + near_rows] for step in (-1, 0, 1)
        )
        return here, before + after

    valid, inverses = inverse_weights(first_row - NEAR, rows, (near_rows, z))
    below, here = design_at(-n), design_at(1 - n)
    for i in range(1 - n, 2 * n - 1):
        above = design_at(i + 1)
        at = first_layer + i
        solid = 1.0 - filtered(below, here, above) * inverse_at(inverses, at, layers)
        below, here = here, above
        conduct = KMIN + (1.0 - KMIN) * (solid * solid * solid)
        conduct_s[i + n - 1] = jnp.where(valid & (at >= 0) & (at < layers), conduct, 0.0)
        if 0 <= i < n:
            solid_ref[i] = solid

    def conduct_at(i):
        return conduct_s[i + n - 1]

    def free_at(i):
        return free_s[i + n - 2]

    for i in range(2 - n, 2 * n - 1):
        pair = conduct_at(i) + conduct_at(i - 1)
        pair = pair + down(pair, 0)
        pair = pair + lower_z(pair)
        free = layer_at(1, i)
        inverse = 1.0 / (free * (pair * (1.0 / 3.0)) + (1.0 - free))
        free_s[i + n - 2] = free
        inverse_s[i + n - 2] = inverse
        u0_s[i + n - 2] = layer_at(2, i) * inverse

    row = lax.broadcasted_iota(jnp.int32, (near_rows, z), 0)
    own = (row >= NEAR) & (row < NEAR + own_rows)
    sums = [jnp.zeros((8, 128), jnp.float32) for _ in range(MOMENTS)]

    def gather(which, product):
        sums[which] = sums[which] + tile_sum(jnp.where(own, product, 0.0))

    def step(previous, first, count):
        for i, image in apply_layers(lambda i: free_at(i) * previous(i), conduct_at, first, count):
            free, start = free_at(i), previous(i)
            image = free * image + (1.0 - free) * start
            yield i, start, image, image * inverse_s[i + n - 2] - start

    for i, start, image, later in step(lambda i: u0_s[i + n - 2], 3 - n, 3 * n - 5):
        u1_s[i + n - 3] = later
        if 0 <= i <= n:
            basis_ref[0, i] = start
        if 0 <= i < n:
            rhs = layer_at(2, i)
            gather(0, start * image)
            gather(1, later * image)
            gather(5, rhs * start)
            gather(6, rhs * later)
    for i, start, image, later in step(lambda i: u1_s[i + n - 3], 0, n + 1):
        basis_ref[1, i] = start
        basis_ref[2, i] = later
        if i < n:
            gather(2, start * image)
            gather(3, later * image)
            gather(7, layer_at(2, i) * later)
    low = yz_modes(free_at(0) * basis_ref[2, 0])
    for i in range(n):
        high = yz_modes(free_at(i + 1) * basis_ref[2, i + 1])
        square = sum(order * value * value for order, value in element_modes(low, high).values())
        last = basis_ref[2, i]
        gather(4, square * (conduct_at(i) * (1.0 / 48.0)) + (1.0 - free_at(i)) * last * last)
        low = high

    table = jnp.concatenate([jnp.sum(partial, axis=0, keepdims=True) for partial in sums], axis=0)
    column = jnp.sum(table, axis=1, keepdims=True)
    diagonal = lax.broadcasted_iota(jnp.int32, (8, 128), 0) == lax.broadcasted_iota(jnp.int32, (8, 128), 1)
    total = jnp.sum(jnp.where(diagonal, column, 0.0), axis=0, keepdims=True)
    moments_ref[...] = jnp.broadcast_to(total, moments_ref.shape)


def integrand_kernel(
    n, own_rows, layers, rows,
    basis_ref, solid_ref, warmth_ref, same_ref, next_ref,
    scaled_ref, to_same_ref, to_next_ref,
):
    even = lax.axis_index("gx") % 2 == 0
    first_layer = lax.axis_index("gx") * n
    first_row = lax.axis_index("gy") * own_rows
    shape = solid_ref.shape[1:]
    places = Layers(n, own_rows, shape[1])
    _, inverses = inverse_weights(first_row - NEAR, rows, shape)
    warm_low = yz_modes(warmth_ref[0])
    lows = [yz_modes(basis_ref[k, 0]) for k in range(BASIS)]
    for i in range(n):
        if i + 1 < n:
            warm = warmth_ref[i + 1]
        else:
            warm = jnp.where(even, spare_rows(places, same_ref), spare_rows(places, next_ref))
        warm_high = yz_modes(warm)
        solid = solid_ref[i]
        share = (3.0 * solid * solid) * inverse_at(inverses, first_layer + i, layers)
        load = {
            key: (order / 48.0) * value for key, (order, value) in element_modes(warm_low, warm_high).items()
        }
        for k in range(BASIS):
            high = yz_modes(basis_ref[k, i + 1])
            modes = element_modes(lows[k], high)
            energy = sum(load[key] * value for key, (_, value) in modes.items())
            total = lows[k][0] + high[0]
            scaled_ref[k, i] = share * ((1.0 - KMIN) * energy - (QZERO / 8.0) * total)
            lows[k] = high
        warm_low = warm_high
    for k in range(BASIS):
        first, last = scaled_ref[k, 0], scaled_ref[k, n - 1]
        to_same_ref[k] = jnp.where(even, last, first)
        to_next_ref[k] = jnp.where(even, first, last)


def spread_kernel(moments_ref, total_ref):
    total = jnp.sum(moments_ref[...], axis=0, keepdims=True)
    total_ref[...] = jnp.broadcast_to(total, total_ref.shape)


def coefficients(total):
    a0, a1, a2, a3, a4, b0, b1, b2 = (
        jnp.broadcast_to(total[:, k : k + 1], (1, 128)) for k in range(MOMENTS)
    )
    l10 = a1 / a0
    l20 = a2 / a0
    d1 = a2 - l10 * a1
    t21 = a3 - l20 * a1
    l21 = t21 / d1
    d2 = a4 - l20 * a2 - l21 * t21
    z1 = b1 - l10 * b0
    z2 = b2 - l20 * b0 - l21 * z1
    y2 = z2 / d2
    y1 = z1 / d1 - l21 * y2
    y0 = b0 / a0 - l10 * y1 - l20 * y2
    return y0, y1, y2


def final_kernel(n, own_rows, moments_ref, basis_ref, scaled_ref, same_ref, next_ref, dual_ref, sens_ref):
    even = lax.axis_index("gx") % 2 == 0
    z = dual_ref.shape[-1]
    near_rows = own_rows + 2 * NEAR
    coefs = [
        jnp.broadcast_to(jnp.concatenate([y] * (z // 128), axis=1), (near_rows, z))
        for y in coefficients(jnp.sum(moments_ref[...], axis=0, keepdims=True))
    ]

    def combined(layers):
        return sum(coef * layer for coef, layer in zip(coefs, layers))

    for i in range(n):
        dual_ref[i] = combined([basis_ref[k, i] for k in range(BASIS)])[NEAR : NEAR + own_rows]
    same = combined([same_ref[k] for k in range(BASIS)])
    other = combined([next_ref[k] for k in range(BASIS)])
    layers = [combined([scaled_ref[k, i] for k in range(BASIS)]) for i in range(n)]
    layers = [jnp.where(even, other, same)] + layers + [jnp.where(even, same, other)]
    layers = [with_rim(layer) for layer in layers]
    for i in range(n):
        sens_ref[i] = filtered(*layers[i : i + 3])[NEAR : NEAR + own_rows]


def shifted(arr, axis, step):
    count = lax.axis_size(axis)
    return lax.ppermute(arr, axis, [(i, i + step) for i in range(count) if 0 <= i + step < count])


def swapped(arr, axis, start):
    pairs = [(i, i + 1) for i in range(start, lax.axis_size(axis) - 1, 2)]
    return lax.ppermute(arr, axis, pairs + [(j, i) for i, j in pairs])


def body(gx, gy, material_fraction, primal_warmth, empty_region_flags, dirichlet_flags):
    n, own_rows, z = material_fraction.shape
    sizes = (n, own_rows, gx * n, gy * own_rows)
    near = own_rows + 2 * NEAR

    def call(name, kernel, outs, *operands, scratch=(), space=pltpu.VMEM, limit=VMEM_LIMIT, flops=0):
        return pl.pallas_call(
            kernel,
            out_shape=[jax.ShapeDtypeStruct(shape, jnp.float32) for shape in outs],
            in_specs=[pl.BlockSpec(memory_space=space)] * len(operands),
            out_specs=[pl.BlockSpec(memory_space=pltpu.VMEM)] * len(outs),
            scratch_shapes=list(scratch),
            compiler_params=pltpu.CompilerParams(vmem_limit_bytes=limit),
            cost_estimate=pl.CostEstimate(flops=flops, bytes_accessed=1 << 20, transcendentals=0),
            name=name,
        )(*operands)

    def floats(*shape):
        return pltpu.VMEM(shape, jnp.float32)

    brick_shape = (n, own_rows, z)
    *own, y_up, y_down = call(
        "load",
        functools.partial(load_kernel, n),
        [brick_shape] * 4 + [(2 * n, 8, z)] * 2,
        material_fraction, primal_warmth, empty_region_flags, dirichlet_flags,
        scratch=[
            floats(*brick_shape),
            pltpu.VMEM(brick_shape, jnp.int32),
            pltpu.VMEM(brick_shape, jnp.int32),
            pltpu.SemaphoreType.DMA((4,)),
        ],
        space=pltpu.HBM,
        limit=LOAD_LIMIT,
    )
    y_low = shifted(y_up, "gy", 1)
    y_high = shifted(y_down, "gy", -1)
    places = Layers(n, own_rows, z)
    free, rhs, warmth, to_same, to_next = call(
        "extend",
        functools.partial(extend_kernel, n, own_rows),
        [(n, near, z)] * 3 + [(places.tiles, 8, z)] * 2,
        *own, y_low, y_high,
    )
    same, other = swapped(to_same, "gx", 0), swapped(to_next, "gx", 1)

    pairs = 2 if gx % 2 == 0 else 1
    inner, outer = pairs * gy, gx // pairs
    moments, basis, solid = call(
        "basis",
        functools.partial(basis_kernel, *sizes),
        [(inner, 128), (BASIS, n + 1, near, z), (n, near, z)],
        to_same, free, rhs, same, other,
        scratch=[floats(count, near, z) for count in (3 * n - 2, 3 * n - 3, 3 * n - 3, 3 * n - 3, 3 * n - 5)],
    )
    scaled, to_same, to_next = call(
        "integrand",
        functools.partial(integrand_kernel, *sizes),
        [(BASIS, n, near, z), (BASIS, near, z), (BASIS, near, z)],
        basis, solid, warmth, same, other,
    )

    near_groups = [
        [(g * pairs + c) * gy + y for c in range(pairs) for y in range(gy)] for g in range(outer)
    ]
    far_groups = [
        [(g * pairs + c) * gy + y for g in range(outer)] for c in range(pairs) for y in range(gy)
    ]
    moments = lax.all_to_all(moments, ("gx", "gy"), 0, 0, axis_index_groups=near_groups, tiled=True)
    (moments,) = call("spread", spread_kernel, [(outer, 128)], moments, flops=FAR_WORK)
    from_same, from_next = swapped(to_same, "gx", 0), swapped(to_next, "gx", 1)
    moments = lax.all_to_all(moments, ("gx", "gy"), 0, 0, axis_index_groups=far_groups, tiled=True)
    return tuple(
        call(
            "combine",
            functools.partial(final_kernel, n, own_rows),
            [brick_shape, brick_shape],
            moments, basis, scaled, from_same, from_next,
        )
    )


def solution(mesh):
    placed = P("gx", "gy", None)
    return jax.shard_map(
        functools.partial(body, mesh.shape["gx"], mesh.shape["gy"]),
        mesh=mesh,
        in_specs=(placed,) * 4,
        out_specs=(placed, placed),
        check_vma=False,
    )
```
